256 devices in a mesh: dp: 64 (over y, z, core), sp: 4 (over x).
Axes of the slice: x: 4, y: 4, z: 8, core: 2. Of those that a mesh axis runs over, the one named last changes fastest.
Arguments:
- normed: bfloat16 [32768, 2560], P(('dp', 'sp')), may hold values from -24 to 24
- w_query: bfloat16 [2560, 4096], P(None, 'sp'), may hold values from -0.125 to 0.125
- key_weight: bfloat16 [2560, 512], P(None, 'sp'), may hold values from -0.125 to 0.125
- value_weight: bfloat16 [2560, 512], P(None, 'sp'), may hold values from -0.125 to 0.125
- q_gain: float32 [128], replicated, may hold values from 0.25 to 1.75
- key_norm_gain: float32 [128], replicated, may hold values from 0.25 to 1.75
- ctx_grad: bfloat16 [32768, 4096], P(('dp', 'sp')), may hold values from -6 to 6
- lengths: int32 [64], P('dp'), may hold values from 64 to 512, as said below
Outputs:
- normed_input_gradient: bfloat16 [32768, 2560], P(('dp', 'sp'))
- grad_w_query: float32 [2560, 4096], P('dp', 'sp')
- grad_w_key: float32 [2560, 512], P('dp', 'sp')
- grad_w_value: float32 [2560, 512], P('dp', 'sp')
The draws below stay inside these ranges and needn't reach their ends.
Inputs may be any that keep to these rules, and one draw needn't show every extreme that they name: `lengths`: in every draw some response has its whole span valid and some only one eighth of 512.
All inputs are finite; a program needn't handle non-finite values.
Results may differ from the reference program's by a relative error of at most 0.008.
Values may be sent and summed in bfloat16 or wider, within the bound.
A program may use at most 128 MiB of HBM per device.

```python
import math
import jax
import jax.numpy as jnp
from jax import lax

INPUT_FEATURES = 2560
QUERY_HEADS = 32
KEY_HEADS = 4
HEAD_SIZE = 128
QUERY_PER_KV = 8
SPAN_TOKENS = 512
RESPONSES = 64
TOKENS = 32768


def draw_lengths(key, part):
    key = jax.random.fold_in(key, 11)
    first_key, second_key = jax.random.split(key)
    drawn = jax.random.randint(first_key, (RESPONSES,), SPAN_TOKENS // 8, SPAN_TOKENS + 1, dtype=jnp.int32)
    chosen = jax.random.permutation(second_key, RESPONSES)
    drawn = drawn.at[chosen[0]].set(SPAN_TOKENS)
    return drawn.at[chosen[1]].set(SPAN_TOKENS // 8)


def strengthened(values, key, source, target, parts, factor):
    def block_of(dim):
        return (jnp.arange(values.shape[dim]) // (values.shape[dim] // parts)).reshape((-1,) + (1,) * (values.ndim - 1 - dim))

    first = jax.random.permutation(key, parts)[block_of(target)]
    second = (block_of(target) + parts // 2) % parts
    return jnp.where((block_of(source) == first) | (block_of(source) == second), factor * values, values)


def shard_levels(rng, dims, shards, least, high):
    loudness, own = 1.0, jax.random.fold_in(rng, 6)
    for dim, shards_of in shards:
        heights = jnp.exp(jax.random.uniform(jax.random.fold_in(own, dim), (shards_of,), jnp.float32, least / len(shards), high / len(shards)))
        loudness = loudness * jnp.repeat(heights, dims[dim] // shards_of).reshape([-1 if axis == dim else 1 for axis in range(len(dims))])
    return loudness


def centred(own_key, extent, deviation, bound, cuts=(), kind=jnp.bfloat16):
    entries = deviation * jax.random.normal(own_key, extent, jnp.float32)
    if cuts:
        entries = entries * shard_levels(own_key, extent, cuts, -0.22, 0.18)
    return jnp.clip(entries, -bound, bound).astype(kind)


def noise_with(rng, shape, spread, most, pieces, heavy, kind=jnp.bfloat16):
    entries = spread * jax.random.normal(rng, shape, jnp.float32)
    if pieces:
        entries = entries * shard_levels(rng, shape, pieces, -0.22, 0.18)
    return jnp.clip(strengthened(entries, jax.random.fold_in(rng, 3), *heavy), -most, most).astype(kind)


def setup_inputs(seed: int = 0) -> dict:
    arg_keys = jax.random.split(jax.random.key(seed), 9)
    return {
        "normed": noise_with(arg_keys[0], (TOKENS, INPUT_FEATURES), 1.0, 24.0, ((0, 256),), (0, 1, 256, 6.0)),
        "w_query": centred(arg_keys[1], (INPUT_FEATURES, QUERY_HEADS * HEAD_SIZE), INPUT_FEATURES ** -0.5, 0.125, ((1, 4),)),
        "key_weight": centred(arg_keys[2], (INPUT_FEATURES, KEY_HEADS * HEAD_SIZE), INPUT_FEATURES ** -0.5, 0.125, ((1, 4),)),
        "value_weight": centred(arg_keys[3], (INPUT_FEATURES, KEY_HEADS * HEAD_SIZE), INPUT_FEATURES ** -0.5, 0.125, ((1, 4),)),
        "q_gain": jnp.clip(1.0 + 0.15 * jax.random.normal(arg_keys[4], (HEAD_SIZE,), jnp.float32), 0.25, 1.75),
        "key_norm_gain": jnp.clip(1.0 + 0.15 * jax.random.normal(arg_keys[5], (HEAD_SIZE,), jnp.float32), 0.25, 1.75),
        "ctx_grad": centred(arg_keys[6], (TOKENS, QUERY_HEADS * HEAD_SIZE), 1.0, 6.0, ((0, 256),)),
        "lengths": draw_lengths(jax.random.fold_in(arg_keys[8], 71), 0),
    }


epsilon = 1e-06
log_base = math.log(1000000.0)

def angle_tables(length, width):
    position = jnp.arange(length, dtype=jnp.int32).astype(jnp.float32)
    freqs = jnp.exp(jnp.arange(width // 2, dtype=jnp.float32) * (-2.0 * log_base / width))
    angles = position[:, None] * freqs[None, :]
    cosine_table = jnp.cos(angles)
    sine_values = jnp.sin(angles)
    return (jnp.concatenate([cosine_table, cosine_table], 1), jnp.concatenate([sine_values, sine_values], 1))

def turned(values):
    half = values.shape[-1] // 2
    return jnp.concatenate([-values[..., half:], values[..., :half]], -1)

def rotate_pairs(values, cosine_table, sine_values):
    return values * cosine_table + turned(values) * sine_values

def inverse_rotation(grads, cosine_table, sine_values):
    return grads * cosine_table - turned(grads) * sine_values

def normalize(values, gain):
    inverse = lax.rsqrt(lax.optimization_barrier(jnp.mean(values * values, -1, keepdims=True)) + epsilon)
    return (values * inverse * gain, inverse)

def head_norm_gradient(values, inverse, gain, grads):
    weighted = gain * grads
    return inverse * weighted - values * (inverse * inverse * inverse) * lax.optimization_barrier(jnp.mean(values * weighted, -1, keepdims=True))

def reference(normed, w_query, key_weight, value_weight, q_gain, key_norm_gain, ctx_grad, lengths):
    scale_factor = HEAD_SIZE ** (-0.5)
    inputs = normed.reshape(RESPONSES, SPAN_TOKENS, INPUT_FEATURES)
    cotangents = ctx_grad.reshape(RESPONSES, SPAN_TOKENS, QUERY_HEADS * HEAD_SIZE)
    positions = jnp.arange(SPAN_TOKENS, dtype=jnp.int32)
    combined_width = (QUERY_HEADS + 2 * KEY_HEADS) * HEAD_SIZE
    cosine_base, sine_base = angle_tables(SPAN_TOKENS, HEAD_SIZE)
    cosine_table = cosine_base[:, None, :]
    sine_values = sine_base[:, None, :]

    def one_response(running_total, response):
        token_rows, output_cotangent, length = response
        q_proj = jnp.dot(token_rows, w_query, preferred_element_type=jnp.float32).reshape(SPAN_TOKENS, QUERY_HEADS, HEAD_SIZE)
        key_projected = jnp.dot(token_rows, key_weight, preferred_element_type=jnp.float32).reshape(SPAN_TOKENS, KEY_HEADS, HEAD_SIZE)
        value_row_block = jnp.dot(token_rows, value_weight, preferred_element_type=jnp.float32).astype(jnp.bfloat16).reshape(SPAN_TOKENS, KEY_HEADS, HEAD_SIZE)
        q_normed, q_inverse = normalize(q_proj, q_gain)
        k_normed, key_inverse_norm = normalize(key_projected, key_norm_gain)
        query_matrix = rotate_pairs(q_normed, cosine_table, sine_values).astype(jnp.bfloat16)
        key_rows = rotate_pairs(k_normed, cosine_table, sine_values).astype(jnp.bfloat16)
        unmasked_rows = positions < length
        allowed = (positions[None, :] <= positions[:, None]) & unmasked_rows[None, :]
        output_gradient = jnp.where(unmasked_rows[:, None], output_cotangent, jnp.zeros((), jnp.bfloat16)).reshape(SPAN_TOKENS, KEY_HEADS, QUERY_PER_KV, HEAD_SIZE)
        query_full_width = query_matrix.reshape(SPAN_TOKENS, KEY_HEADS, QUERY_PER_KV, HEAD_SIZE).astype(jnp.float32)
        key_wide = key_rows.astype(jnp.float32)
        value_wide = value_row_block.astype(jnp.float32)
        gradient_full_width = output_gradient.astype(jnp.float32)
        scores = jnp.einsum('ikgd,jkd->kgij', query_full_width, key_wide) * scale_factor
        weights = jnp.where(allowed, jnp.exp(scores), jnp.zeros((), jnp.float32))
        probs = weights / lax.optimization_barrier(jnp.sum(weights, -1, keepdims=True))
        probabilities_reduced = lax.optimization_barrier(probs.astype(jnp.bfloat16)).astype(jnp.float32)
        context = jnp.einsum('kgij,jkd->ikgd', probabilities_reduced, value_wide)
        delta = lax.optimization_barrier(jnp.sum(gradient_full_width * context, -1))
        dprob = jnp.einsum('ikgd,jkd->kgij', gradient_full_width, value_wide)
        dscore = probs * (dprob - jnp.transpose(delta, (1, 2, 0))[..., None])
        dscore_low = lax.optimization_barrier(dscore.astype(jnp.bfloat16)).astype(jnp.float32)
        dq_rot = jnp.einsum('kgij,jkd->ikgd', dscore_low, key_wide).reshape(SPAN_TOKENS, QUERY_HEADS, HEAD_SIZE) * scale_factor
        rotated_key_gradient = jnp.einsum('lufr,flux->rlx', dscore_low, query_full_width) * scale_factor
        value_gradient = jnp.einsum('lufr,flux->rlx', probabilities_reduced, gradient_full_width).astype(jnp.bfloat16).reshape(SPAN_TOKENS, KEY_HEADS * HEAD_SIZE)
        query_grad = head_norm_gradient(q_proj, q_inverse, q_gain, inverse_rotation(dq_rot, cosine_table, sine_values)).astype(jnp.bfloat16).reshape(SPAN_TOKENS, QUERY_HEADS * HEAD_SIZE)
        key_gradient = head_norm_gradient(key_projected, key_inverse_norm, key_norm_gain, inverse_rotation(rotated_key_gradient, cosine_table, sine_values)).astype(jnp.bfloat16).reshape(SPAN_TOKENS, KEY_HEADS * HEAD_SIZE)
        input_grad = jnp.dot(query_grad, w_query.T, preferred_element_type=jnp.float32)
        input_grad = input_grad + jnp.dot(key_gradient, key_weight.T, preferred_element_type=jnp.float32)
        input_grad = input_grad + jnp.dot(value_gradient, value_weight.T, preferred_element_type=jnp.float32)
        stacked = jnp.concatenate([query_grad, key_gradient, value_gradient], 1)
        running_total = running_total + jnp.dot(token_rows.T, stacked, preferred_element_type=jnp.float32)
        return (running_total, input_grad.astype(jnp.bfloat16))
    running_total, input_grads = lax.scan(one_response, jnp.zeros((INPUT_FEATURES, combined_width), jnp.float32), (inputs, cotangents, lengths))
    normed_input_gradient = input_grads.reshape(RESPONSES * SPAN_TOKENS, INPUT_FEATURES)
    return (normed_input_gradient, running_total[:, :QUERY_HEADS * HEAD_SIZE], running_total[:, QUERY_HEADS * HEAD_SIZE:(QUERY_HEADS + KEY_HEADS) * HEAD_SIZE], running_total[:, (QUERY_HEADS + KEY_HEADS) * HEAD_SIZE:])
```

```python
import math

import jax
import jax.numpy as jnp
import numpy as np
from jax import lax
from jax.experimental import pallas as pl
from jax.experimental.pallas import tpu as pltpu
from jax.sharding import PartitionSpec as P

F32 = jnp.float32
BF16 = jnp.bfloat16
EPSILON = 1e-06
LOG_BASE = math.log(1000000.0)
RING_X, RING_Y, RING_Z = 4, 4, 8
ROWS = 128
SPAN = 512
FEATURES = 2560
HEADS = 8
HEAD = 128
QUERY_COLUMNS = HEADS * HEAD
COLUMNS = QUERY_COLUMNS + 2 * HEAD
PAIR = 2 * HEAD
TILES = COLUMNS // PAIR
BLOCKS = RING_Y * RING_Z
BLOCK_ROWS = FEATURES // BLOCKS
SHARE = BLOCK_ROWS // 2
SCALE = HEAD**-0.5
SCORE_SCALE = SCALE * math.log2(math.e)
QUERY_ROWS = 256

GATHER = 0
CONTEXT = GATHER + 6
CORE = CONTEXT + 3 * (TILES - 1)
Y_SLOT = CORE + TILES
Z_SLOT = Y_SLOT + 6 * TILES
FINAL = Z_SLOT + 7 * TILES
INPUT = FINAL + 1
SLOTS = INPUT + 6


def angle_tables():
    position = np.arange(SPAN, dtype=np.float32)
    freqs = np.exp(np.arange(HEAD // 2, dtype=np.float32) * np.float32(-2.0 * LOG_BASE / HEAD))
    angles = position[:, None] * freqs.astype(np.float32)[None, :]
    cosine, sine = np.cos(angles), np.sin(angles)
    return (
        np.concatenate([cosine, cosine], 1).astype(np.float32),
        np.concatenate([-sine, sine], 1).astype(np.float32),
    )


def dot(a, b):
    return jnp.dot(a, b, preferred_element_type=F32)


def dot_t(a, b):
    return lax.dot_general(a, b, (((1,), (1,)), ((), ())), preferred_element_type=F32)


def half_turn(a):
    return pltpu.roll(a, HEAD // 2, 1)


def head_mean(a):
    return jnp.sum(a, -1, keepdims=True) * (1.0 / HEAD)


def aligned(index, unit):
    return pl.multiple_of(index * unit, unit)


def kernel(
    normed, w_query, key_weight, value_weight, q_gain, k_gain, ctx_in, lengths, cosine, sine,
    dx_out, gq_out, gk_out, gv_out,
    weights, span, span_t, ctx, u_query, u_key, queries, queries_t, keys, values,
    grads, dk_t, dv_t,
    part, part_send, part_recv, y_far_r, y_far_l, y_near_r, y_near_l,
    z_total, z_send_r, z_send_l, z_recv_r, z_recv_l, result, result_recv,
    dx_far, dx_send_r, dx_send_l, dx_wait_r, dx_wait_l, dx_own,
    x_far_r, x_far_l, x_near_r, x_near_l,
    local_sem, send_sem, recv_sem,
):
    dp = lax.axis_index("dp")
    x = lax.axis_index("sp")
    core = lax.rem(dp, 2)
    z = lax.rem(lax.div(dp, 2), RING_Z)
    y = lax.div(dp, 2 * RING_Z)

    def place(y_at, z_at, core_at):
        return (y_at * RING_Z + z_at) * 2 + core_at

    x_next, x_prev, x_far = lax.rem(x + 1, RING_X), lax.rem(x + 3, RING_X), lax.rem(x + 2, RING_X)
    y_next, y_prev, y_far = lax.rem(y + 1, RING_Y), lax.rem(y + 3, RING_Y), lax.rem(y + 2, RING_Y)
    z_next, z_prev = lax.rem(z + 1, RING_Z), lax.rem(z + RING_Z - 1, RING_Z)
    to_xr, to_xl, to_xf = (dp, x_next), (dp, x_prev), (dp, x_far)
    to_yr, to_yl = (place(y_next, z, core), x), (place(y_prev, z, core), x)
    to_zr, to_zl = (place(y, z_next, core), x), (place(y, z_prev, core), x)
    to_core = (place(y, z, 1 - core), x)

    def remote(src, dst, slot, device):
        return pltpu.make_async_remote_copy(
            src_ref=src,
            dst_ref=dst,
            send_sem=send_sem.at[slot],
            recv_sem=recv_sem.at[slot],
            device_id=device,
            device_id_type=pl.DeviceIdType.MESH,
        )

    own_rows = pltpu.make_async_copy(normed, span.at[x], local_sem.at[0])
    own_weights = [
        pltpu.make_async_copy(w_query, weights.at[:, pl.ds(0, QUERY_COLUMNS)], local_sem.at[1]),
        pltpu.make_async_copy(
            key_weight, weights.at[:, pl.ds(QUERY_COLUMNS, HEAD)], local_sem.at[2]
        ),
        pltpu.make_async_copy(
            value_weight, weights.at[:, pl.ds(QUERY_COLUMNS + HEAD, HEAD)], local_sem.at[3]
        ),
    ]
    own_context = pltpu.make_async_copy(
        ctx_in.at[:, pl.ds(aligned(x, QUERY_COLUMNS), QUERY_COLUMNS)],
        ctx.at[pl.ds(aligned(x, ROWS), ROWS), :],
        local_sem.at[4],
    )
    own_rows.start()
    for copy in own_weights:
        copy.start()
    own_context.start()

    barrier = pltpu.get_barrier_semaphore()
    for device in (to_xr, to_xl, to_xf, to_yr, to_yl, to_zr, to_zl, to_core):
        pl.semaphore_signal(barrier, inc=1, device_id=device, device_id_type=pl.DeviceIdType.MESH)
    pl.semaphore_wait(barrier, 8)

    low, high = pl.ds(0, ROWS // 2), pl.ds(ROWS // 2, ROWS // 2)

    def gather_own(slot, half, device):
        return remote(normed.at[half, :], span.at[x, half, :], GATHER + slot, device)

    def gather_pass(slot, owner, half, device):
        return remote(
            span.at[owner, half, :], span.at[owner, half, :], GATHER + slot, device
        )

    right_low, right_high = gather_own(0, low, to_xr), gather_own(1, high, to_xr)
    left_high, left_low = gather_own(2, high, to_xl), gather_own(3, low, to_xl)
    pass_right = gather_pass(4, x_prev, low, to_xr)
    pass_left = gather_pass(5, x_next, high, to_xl)
    right_low.start()
    left_high.start()
    right_high.start()
    left_low.start()

    def context_copy(tile, slot, owner, device):
        start = pl.multiple_of(owner * QUERY_COLUMNS + tile * PAIR, PAIR)
        return remote(
            ctx_in.at[:, pl.ds(start, PAIR)],
            ctx.at[pl.ds(aligned(x, ROWS), ROWS), pl.ds(aligned(tile, PAIR), PAIR)],
            CONTEXT + 3 * tile + slot,
            device,
        )

    def context_copies(tile):
        return (
            context_copy(tile, 0, x_next, to_xr),
            context_copy(tile, 1, x_prev, to_xl),
            context_copy(tile, 2, x_far, to_xf),
        )

    def rotated(u, gain, cos, sin):
        normal = u * lax.rsqrt(head_mean(u * u) + EPSILON) * gain
        return normal * cos + half_turn(normal) * sin

    def project(block):
        rows = pl.ds(aligned(block, ROWS), ROWS)

        def pair(tile, carry):
            out = dot(span[block], weights[:, pl.ds(aligned(tile, PAIR), PAIR)])
            for side in range(2):
                u = out[:, side * HEAD : (side + 1) * HEAD]
                head = 2 * tile + side
                u_query[head, rows, :] = u
                turned = rotated(u, q_gain[...], cosine[rows, :], sine[rows, :])
                queries[head, rows, :] = turned.astype(BF16)
                queries_t[head, :, rows] = turned.T.astype(BF16)
            return carry

        lax.fori_loop(0, HEADS // 2, pair, 0)
        out = dot(span[block], weights[:, QUERY_COLUMNS:])
        u = out[:, :HEAD]
        u_key[rows, :] = u
        keys[rows, :] = rotated(u, k_gain[...], cosine[rows, :], sine[rows, :]).astype(BF16)
        values[rows, :] = out[:, HEAD:].astype(BF16)

    def transpose_rows(block):
        def chunk(i, carry):
            features = pl.ds(aligned(i, 256), 256)
            columns = pl.ds(aligned(block, ROWS), ROWS)
            span_t[features, columns] = span[block, :, features].astype(F32).T.astype(BF16)
            return carry

        lax.fori_loop(0, FEATURES // 256, chunk, 0)

    own_rows.wait()
    for copy in own_weights:
        copy.wait()
    project(x)
    right_low.wait_recv()
    left_high.wait_recv()
    pass_right.start()
    pass_left.start()

    def send_context(tile, carry):
        for copy in context_copies(tile):
            copy.start()
        return carry

    lax.fori_loop(0, TILES - 1, send_context, 0)
    transpose_rows(x)
    right_high.wait_recv()
    project(x_prev)
    left_low.wait_recv()
    project(x_next)
    transpose_rows(x_prev)
    transpose_rows(x_next)
    pass_right.wait_recv()
    pass_left.wait_recv()
    project(x_far)
    transpose_rows(x_far)
    own_context.wait()

    length = lengths[0]

    def norm_gradient(u, gain, grad):
        inverse = lax.rsqrt(head_mean(u * u) + EPSILON)
        weighted = gain * grad
        return inverse * weighted - u * (inverse * inverse * inverse) * head_mean(u * weighted)

    def unrotated(grad, rows):
        return grad * cosine[rows, :] - half_turn(grad) * sine[rows, :]

    def attend(head):
        columns = pl.ds(aligned(head, HEAD), HEAD)
        for first in range(0, SPAN, QUERY_ROWS):
            rows = slice(first, first + QUERY_ROWS)
            seen = first + QUERY_ROWS
            position = lax.broadcasted_iota(jnp.int32, (QUERY_ROWS, 1), 0) + first
            limit = jnp.minimum(position, length - 1)
            key_position = lax.broadcasted_iota(jnp.int32, (QUERY_ROWS, seen), 1)
            key, value = keys[:seen, :], values[:seen, :]
            scores = dot_t(queries[head, rows, :], key)
            weight = jnp.where(key_position <= limit, jnp.exp2(scores * SCORE_SCALE), 0.0)
            probs = weight * (1.0 / jnp.sum(weight, -1, keepdims=True))
            probs_low = probs.astype(BF16)
            context = dot(probs_low, value)
            d_out = jnp.where(position < length, ctx[rows, columns].astype(F32), 0.0)
            d_low = d_out.astype(BF16)
            delta = jnp.sum(d_out * context, -1, keepdims=True)
            d_score = (probs * (dot_t(d_low, value) - delta)).astype(BF16)
            d_query = dot(d_score, key) * SCALE
            grads[rows, columns] = norm_gradient(
                u_query[head, rows, :], q_gain[...], unrotated(d_query, rows)
            ).astype(BF16)
            dk_t[:, :seen] += dot(queries_t[head, :, rows], d_score)
            dv_t[:, :seen] += dot(d_out.T.astype(BF16), probs_low)

    dk_t[...] = jnp.zeros_like(dk_t)
    dv_t[...] = jnp.zeros_like(dv_t)

    def attend_pair(tile):
        for copy in context_copies(tile):
            copy.wait_recv()
        for side in range(2):
            attend(2 * tile + side)

    def key_value_gradients():
        d_key = dk_t[...].T * SCALE
        grads[:, QUERY_COLUMNS : QUERY_COLUMNS + HEAD] = norm_gradient(
            u_key[...], k_gain[...], unrotated(d_key, slice(0, SPAN))
        ).astype(BF16)
        grads[:, QUERY_COLUMNS + HEAD :] = dv_t[...].T.astype(BF16)

    def input_part(block, store):
        def chunk(i, carry):
            features = pl.ds(aligned(i, 256), 256)
            rows = grads[pl.ds(aligned(block, ROWS), ROWS), :]
            store(features, dot_t(rows, weights[features, :]))
            return carry

        lax.fori_loop(0, FEATURES // 256, chunk, 0)

    half = ROWS // 2
    input_copies = [
        remote(dx_far.at[low, :], x_far_r, INPUT, to_xr),
        remote(dx_far.at[high, :], x_far_l, INPUT + 1, to_xl),
        remote(dx_send_r.at[high, :], x_near_r.at[high, :], INPUT + 2, to_xr),
        remote(dx_send_l.at[low, :], x_near_l.at[low, :], INPUT + 3, to_xl),
        remote(dx_send_r.at[low, :], x_near_r.at[low, :], INPUT + 4, to_xr),
        remote(dx_send_l.at[high, :], x_near_l.at[high, :], INPUT + 5, to_xl),
    ]

    def input_first():
        def store_far(features, out):
            dx_far[:, features] = out.astype(BF16)

        def store_next(features, out):
            dx_wait_r[:, features] = out[:half]
            dx_send_r[half:, features] = out[half:].astype(BF16)

        def store_prev(features, out):
            dx_wait_l[:, features] = out[half:]
            dx_send_l[:half, features] = out[:half].astype(BF16)

        input_part(x_far, store_far)
        input_copies[0].start()
        input_copies[1].start()
        input_part(x_next, store_next)
        input_copies[2].start()
        input_part(x_prev, store_prev)
        input_copies[3].start()

    def input_own():
        def store_own(features, out):
            dx_own[:, features] = out

        input_part(x, store_own)

    def input_second():
        def chunk(i, carry):
            features = pl.ds(aligned(i, 256), 256)
            dx_send_r[:half, features] = (
                dx_wait_r[:, features] + x_far_r[:, features].astype(F32)
            ).astype(BF16)
            dx_send_l[half:, features] = (
                dx_wait_l[:, features] + x_far_l[:, features].astype(F32)
            ).astype(BF16)
            return carry

        input_copies[0].wait_recv()
        input_copies[1].wait_recv()
        lax.fori_loop(0, FEATURES // 256, chunk, 0)
        input_copies[4].start()
        input_copies[5].start()

    def input_last():
        def chunk(i, carry):
            features = pl.ds(aligned(i, 256), 256)
            dx_out[:, features] = (
                dx_own[:, features]
                + x_near_r[:, features].astype(F32)
                + x_near_l[:, features].astype(F32)
            ).astype(BF16)
            return carry

        for copy in input_copies[2:]:
            copy.wait_recv()
        lax.fori_loop(0, FEATURES // 256, chunk, 0)

    def core_copy(tile):
        return remote(part_send.at[tile], part_recv.at[tile], CORE + tile, to_core)

    chunk_blocks = 4

    def weight_gradient(tile):
        columns = pl.ds(aligned(tile, PAIR), PAIR)

        def chunk(i, carry):
            features = pl.ds(aligned(i, chunk_blocks * BLOCK_ROWS), chunk_blocks * BLOCK_ROWS)
            out = dot(span_t[features, :], grads[:, columns])
            kept = jnp.where(core == 0, out[:, :HEAD], out[:, HEAD:])
            sent = jnp.where(core == 0, out[:, HEAD:], out[:, :HEAD])
            blocks = pl.ds(i * chunk_blocks, chunk_blocks)
            shape = (chunk_blocks, BLOCK_ROWS, HEAD)
            part[tile, blocks] = kept.astype(BF16).reshape(shape)
            part_send[tile, blocks] = sent.astype(BF16).reshape(shape)
            return carry

        lax.fori_loop(0, BLOCKS // chunk_blocks, chunk, 0)
        core_copy(tile).start()

    half_z = RING_Z // 2

    def y_copies(tile):
        slot = Y_SLOT + 6 * tile

        def blocks(y_at, half_at):
            return part.at[tile, pl.ds(y_at * RING_Z + half_at * half_z, half_z)]

        first, second = pl.ds(0, half_z), pl.ds(half_z, half_z)
        return [
            remote(blocks(y_far, 0), y_far_r.at[tile], slot, to_yr),
            remote(blocks(y_far, 1), y_far_l.at[tile], slot + 1, to_yl),
            remote(blocks(y_next, 1), y_near_r.at[tile, second], slot + 2, to_yr),
            remote(blocks(y_prev, 0), y_near_l.at[tile, first], slot + 3, to_yl),
            remote(blocks(y_next, 0), y_near_r.at[tile, first], slot + 4, to_yr),
            remote(blocks(y_prev, 1), y_near_l.at[tile, second], slot + 5, to_yl),
        ]

    def y_first(tile):
        core_copy(tile).wait_recv()

        def add(i, carry):
            blocks = pl.ds(i * chunk_blocks, chunk_blocks)
            total = part[tile, blocks].astype(F32) + part_recv[tile, blocks].astype(F32)
            part[tile, blocks] = total.astype(BF16)
            return carry

        lax.fori_loop(0, BLOCKS // chunk_blocks, add, 0)
        for copy in y_copies(tile)[:4]:
            copy.start()

    def y_second(tile):
        copies = y_copies(tile)
        copies[0].wait_recv()
        copies[1].wait_recv()
        right = pl.ds(y_next * RING_Z, half_z)
        left = pl.ds(y_prev * RING_Z + half_z, half_z)
        part[tile, right] = (part[tile, right].astype(F32) + y_far_r[tile].astype(F32)).astype(BF16)
        part[tile, left] = (part[tile, left].astype(F32) + y_far_l[tile].astype(F32)).astype(BF16)
        copies[4].start()
        copies[5].start()

    def z_copy_right(tile, step):
        return remote(
            z_send_r.at[tile, step], z_recv_r.at[tile, step], Z_SLOT + 7 * tile + step, to_zr
        )

    def z_copy_left(tile, step):
        return remote(
            z_send_l.at[tile, step], z_recv_l.at[tile, step], Z_SLOT + 7 * tile + 4 + step, to_zl
        )

    def z_step(tile, step):
        ahead = z_total[tile, lax.rem(z + 4 - step, RING_Z)]
        if step > 0:
            z_copy_right(tile, step - 1).wait_recv()
            ahead = ahead + z_recv_r[tile, step - 1].astype(F32)
        z_send_r[tile, step] = ahead.astype(BF16)
        z_copy_right(tile, step).start()
        if step < 3:
            behind = z_total[tile, lax.rem(z + RING_Z - 3 + step, RING_Z)]
            if step > 0:
                z_copy_left(tile, step - 1).wait_recv()
                behind = behind + z_recv_l[tile, step - 1].astype(F32)
            z_send_l[tile, step] = behind.astype(BF16)
            z_copy_left(tile, step).start()

    def z_first(tile):
        for copy in y_copies(tile)[2:]:
            copy.wait_recv()

        def add(i, carry):
            z_total[tile, i] = (
                part[tile, y * RING_Z + i].astype(F32)
                + y_near_r[tile, i].astype(F32)
                + y_near_l[tile, i].astype(F32)
            )
            return carry

        lax.fori_loop(0, RING_Z, add, 0)
        z_step(tile, 0)

    def z_last(tile):
        z_copy_right(tile, 3).wait_recv()
        z_copy_left(tile, 2).wait_recv()
        total = (
            z_total[tile, z]
            + z_recv_r[tile, 3].astype(F32)
            + z_recv_l[tile, 2].astype(F32)
        )
        result[0, tile] = total[:SHARE]
        result[1, tile] = total[SHARE:]

    stages = [
        y_first,
        y_second,
        z_first,
        lambda tile: z_step(tile, 1),
        lambda tile: z_step(tile, 2),
        lambda tile: z_step(tile, 3),
        z_last,
    ]

    def step(turn, carry):
        @pl.when(turn < TILES - 1)
        def _():
            attend_pair(turn)

        @pl.when(turn == TILES - 1)
        def _():
            key_value_gradients()
            input_first()

        @pl.when(turn < TILES)
        def _():
            weight_gradient(turn)

        for late, stage in enumerate(stages, 1):

            @pl.when((turn >= late) & (turn < late + TILES))
            def _(late=late, stage=stage):
                stage(turn - late)

        @pl.when(turn == TILES)
        def _():
            input_own()

        @pl.when(turn == TILES + 2)
        def _():
            input_second()

        return carry

    lax.fori_loop(0, TILES + len(stages), step, 0)

    final = remote(result.at[1 - core], result_recv, FINAL, to_core)
    final.start()
    input_last()
    final.wait_recv()

    mine, other = aligned(core, HEAD), aligned(1 - core, HEAD)
    for tile in range(TILES - 1):
        gq_out[:, pl.ds(tile * PAIR + mine, HEAD)] = result[core, tile]
        gq_out[:, pl.ds(tile * PAIR + other, HEAD)] = result_recv[tile]
    kept, received = result[core, TILES - 1], result_recv[TILES - 1]
    gk_out[...] = jnp.where(core == 0, kept, received)
    gv_out[...] = jnp.where(core == 0, received, kept)

    for copy in (right_low, right_high, left_high, left_low, pass_right, pass_left, final):
        copy.wait_send()
    for copy in input_copies:
        copy.wait_send()

    def drain_context(tile, carry):
        for copy in context_copies(tile):
            copy.wait_send()
        return carry

    def drain(tile, carry):
        core_copy(tile).wait_send()
        for copy in y_copies(tile):
            copy.wait_send()
        for index in range(4):
            z_copy_right(tile, index).wait_send()
        for index in range(3):
            z_copy_left(tile, index).wait_send()
        return carry

    lax.fori_loop(0, TILES - 1, drain_context, 0)
    lax.fori_loop(0, TILES, drain, 0)


def local(normed, w_query, key_weight, value_weight, q_gain, key_norm_gain, ctx_grad, lengths):
    cosine, sine = angle_tables()
    block = (BLOCK_ROWS, HEAD)
    vmem = pl.BlockSpec(memory_space=pltpu.VMEM)
    anywhere = pl.BlockSpec(memory_space=pl.ANY)
    smem = pl.BlockSpec(memory_space=pltpu.SMEM)
    scratch = [
        pltpu.VMEM((FEATURES, COLUMNS), BF16),
        pltpu.VMEM((RING_X, ROWS, FEATURES), BF16),
        pltpu.VMEM((FEATURES, SPAN), BF16),
        pltpu.VMEM((SPAN, QUERY_COLUMNS), BF16),
        pltpu.VMEM((HEADS, SPAN, HEAD), F32),
        pltpu.VMEM((SPAN, HEAD), F32),
        pltpu.VMEM((HEADS, SPAN, HEAD), BF16),
        pltpu.VMEM((HEADS, HEAD, SPAN), BF16),
        pltpu.VMEM((SPAN, HEAD), BF16),
        pltpu.VMEM((SPAN, HEAD), BF16),
        pltpu.VMEM((SPAN, COLUMNS), BF16),
        pltpu.VMEM((HEAD, SPAN), F32),
        pltpu.VMEM((HEAD, SPAN), F32),
        pltpu.VMEM((TILES, BLOCKS) + block, BF16),
        pltpu.VMEM((TILES, BLOCKS) + block, BF16),
        pltpu.VMEM((TILES, BLOCKS) + block, BF16),
        pltpu.VMEM((TILES, RING_Z // 2) + block, BF16),
        pltpu.VMEM((TILES, RING_Z // 2) + block, BF16),
        pltpu.VMEM((TILES, RING_Z) + block, BF16),
        pltpu.VMEM((TILES, RING_Z) + block, BF16),
        pltpu.VMEM((TILES, RING_Z) + block, F32),
        pltpu.VMEM((TILES, 4) + block, BF16),
        pltpu.VMEM((TILES, 3) + block, BF16),
        pltpu.VMEM((TILES, 4) + block, BF16),
        pltpu.VMEM((TILES, 3) + block, BF16),
        pltpu.VMEM((2, TILES, SHARE, HEAD), F32),
        pltpu.VMEM((TILES, SHARE, HEAD), F32),
        pltpu.VMEM((ROWS, FEATURES), BF16),
        pltpu.VMEM((ROWS, FEATURES), BF16),
        pltpu.VMEM((ROWS, FEATURES), BF16),
        pltpu.VMEM((ROWS // 2, FEATURES), F32),
        pltpu.VMEM((ROWS // 2, FEATURES), F32),
        pltpu.VMEM((ROWS, FEATURES), F32),
        pltpu.VMEM((ROWS // 2, FEATURES), BF16),
        pltpu.VMEM((ROWS // 2, FEATURES), BF16),
        pltpu.VMEM((ROWS, FEATURES), BF16),
        pltpu.VMEM((ROWS, FEATURES), BF16),
        pltpu.SemaphoreType.DMA((5,)),
        pltpu.SemaphoreType.DMA((SLOTS,)),
        pltpu.SemaphoreType.DMA((SLOTS,)),
    ]
    return pl.pallas_call(
        kernel,
        out_shape=(
            jax.ShapeDtypeStruct((ROWS, FEATURES), BF16),
            jax.ShapeDtypeStruct((SHARE, QUERY_COLUMNS), F32),
            jax.ShapeDtypeStruct((SHARE, HEAD), F32),
            jax.ShapeDtypeStruct((SHARE, HEAD), F32),
        ),
        in_specs=[anywhere] * 4 + [vmem] * 2 + [anywhere, smem] + [vmem] * 2,
        out_specs=(vmem,) * 4,
        scratch_shapes=scratch,
        compiler_params=pltpu.CompilerParams(
            collective_id=0, has_side_effects=True, vmem_limit_bytes=60 * 2**20
        ),
    )(
        normed,
        w_query,
        key_weight,
        value_weight,
        q_gain.reshape(1, HEAD),
        key_norm_gain.reshape(1, HEAD),
        ctx_grad,
        lengths,
        cosine,
        sine,
    )


def solution(mesh):
    in_specs = (
        P(("dp", "sp"), None),
        P(None, "sp"),
        P(None, "sp"),
        P(None, "sp"),
        P(),
        P(),
        P(("dp", "sp"), None),
        P("dp"),
    )
    out_specs = (P(("dp", "sp"), None), P("dp", "sp"), P("dp", "sp"), P("dp", "sp"))
    return jax.shard_map(local, mesh=mesh, in_specs=in_specs, out_specs=out_specs, check_vma=False)
```

```python
import math

import jax
import jax.numpy as jnp
import numpy as np
from jax import lax
from jax.experimental import pallas as pl
from jax.experimental.pallas import tpu as pltpu
from jax.sharding import PartitionSpec as P

F32 = jnp.float32
BF16 = jnp.bfloat16
EPSILON = 1e-06
LOG_BASE = math.log(1000000.0)
RING_X, RING_Y, RING_Z = 4, 4, 8
ROWS = 128
SPAN = 512
FEATURES = 2560
HEADS = 8
HEAD = 128
QUERY_COLUMNS = HEADS * HEAD
COLUMNS = QUERY_COLUMNS + 2 * HEAD
PAIR = 2 * HEAD
TILES = COLUMNS // PAIR
BLOCKS = RING_Y * RING_Z
BLOCK_ROWS = FEATURES // BLOCKS
SHARE = BLOCK_ROWS // 2
SCALE = HEAD**-0.5
SCORE_SCALE = SCALE * math.log2(math.e)
QUERY_ROWS = 256
RINGED = (0, 2)
STRAIGHT = (1, 3, 4)

GATHER = 0
CONTEXT = GATHER + 6
CORE = CONTEXT + 3 * (TILES - 1)
RING_SLOT = CORE + TILES
FINAL = RING_SLOT + 10 * TILES
INPUT = FINAL + 1
SLOTS = INPUT + 10


def angle_tables():
    position = np.arange(SPAN, dtype=np.float32)
    freqs = np.exp(np.arange(HEAD // 2, dtype=np.float32) * np.float32(-2.0 * LOG_BASE / HEAD))
    angles = position[:, None] * freqs.astype(np.float32)[None, :]
    cosine, sine = np.cos(angles), np.sin(angles)
    return (
        np.concatenate([cosine, cosine], 1).astype(np.float32),
        np.concatenate([-sine, sine], 1).astype(np.float32),
    )


def dot(a, b):
    return jnp.dot(a, b, preferred_element_type=F32)


def dot_t(a, b):
    return lax.dot_general(a, b, (((1,), (1,)), ((), ())), preferred_element_type=F32)


def half_turn(a):
    return pltpu.roll(a, HEAD // 2, 1)


def head_mean(a):
    return jnp.sum(a, -1, keepdims=True) * (1.0 / HEAD)


def aligned(index, unit):
    return pl.multiple_of(index * unit, unit)


def kernel(
    normed, w_query, key_weight, value_weight, q_gain, k_gain, ctx_in, lengths, cosine_in, sine_in,
    dx_out, gq_out, gk_out, gv_out,
    cosine, sine, weights, weights_t, span, span_t, ctx, u_query, u_key, queries, queries_t, keys, values,
    grads, dk_t, dv_t,
    part, part_send, part_recv, y_recv, z_send, z_recv,
    long_send, long_recv, short_send, short_recv, last_send, last_recv,
    own_total, result, result_recv,
    dx_far, dx_send_r, dx_send_l, dx_wait_r, dx_wait_l, dx_own,
    x_far_r, x_far_l, x_near_r, x_near_l,
    local_sem, send_sem, recv_sem,
):
    dp = lax.axis_index("dp")
    x = lax.axis_index("sp")
    core = lax.rem(dp, 2)
    z = lax.rem(lax.div(dp, 2), RING_Z)
    y = lax.div(dp, 2 * RING_Z)

    def place(y_at, z_at, core_at):
        return (y_at * RING_Z + z_at) * 2 + core_at

    x_next, x_prev, x_far = lax.rem(x + 1, RING_X), lax.rem(x + 3, RING_X), lax.rem(x + 2, RING_X)
    to_xr, to_xl, to_xf = (dp, x_next), (dp, x_prev), (dp, x_far)
    to_core = (place(y, z, 1 - core), x)
    partners = [to_xr, to_xl, to_xf, to_core]
    partners += [(place(lax.rem(y + k, RING_Y), z, core), x) for k in range(1, RING_Y)]
    partners += [(place(y, lax.rem(z + k, RING_Z), core), x) for k in range(1, RING_Z)]

    def remote(src, dst, slot, device):
        return pltpu.make_async_remote_copy(
            src_ref=src,
            dst_ref=dst,
            send_sem=send_sem.at[slot],
            recv_sem=recv_sem.at[slot],
            device_id=device,
            device_id_type=pl.DeviceIdType.MESH,
        )

    own_rows = pltpu.make_async_copy(normed, span.at[x], local_sem.at[0])
    own_weights = [
        pltpu.make_async_copy(w_query, weights.at[:, pl.ds(0, QUERY_COLUMNS)], local_sem.at[1]),
        pltpu.make_async_copy(
            key_weight, weights.at[:, pl.ds(QUERY_COLUMNS, HEAD)], local_sem.at[2]
        ),
        pltpu.make_async_copy(
            value_weight, weights.at[:, pl.ds(QUERY_COLUMNS + HEAD, HEAD)], local_sem.at[3]
        ),
    ]
    own_context = pltpu.make_async_copy(
        ctx_in.at[:, pl.ds(aligned(x, QUERY_COLUMNS), QUERY_COLUMNS)],
        ctx.at[pl.ds(aligned(x, ROWS), ROWS), :],
        local_sem.at[4],
    )
    tables = [
        pltpu.make_async_copy(cosine_in, cosine, local_sem.at[5]),
        pltpu.make_async_copy(sine_in, sine, local_sem.at[6]),
    ]
    own_rows.start()
    for copy in own_weights + tables:
        copy.start()
    own_context.start()

    barrier = pltpu.get_barrier_semaphore()
    for device in partners:
        pl.semaphore_signal(barrier, inc=1, device_id=device, device_id_type=pl.DeviceIdType.MESH)
    pl.semaphore_wait(barrier, len(partners))

    low, high = pl.ds(0, ROWS // 2), pl.ds(ROWS // 2, ROWS // 2)

    def gather_own(slot, half, device):
        return remote(normed.at[half, :], span.at[x, half, :], GATHER + slot, device)

    def gather_pass(slot, owner, half, device):
        return remote(
            span.at[owner, half, :], span.at[owner, half, :], GATHER + slot, device
        )

    right_low, right_high = gather_own(0, low, to_xr), gather_own(1, high, to_xr)
    left_high, left_low = gather_own(2, high, to_xl), gather_own(3, low, to_xl)
    pass_right = gather_pass(4, x_prev, low, to_xr)
    pass_left = gather_pass(5, x_next, high, to_xl)
    right_low.start()
    left_high.start()
    right_high.start()
    left_low.start()

    def context_copy(tile, slot, owner, device):
        start = pl.multiple_of(owner * QUERY_COLUMNS + tile * PAIR, PAIR)
        return remote(
            ctx_in.at[:, pl.ds(start, PAIR)],
            ctx.at[pl.ds(aligned(x, ROWS), ROWS), pl.ds(aligned(tile, PAIR), PAIR)],
            CONTEXT + 3 * tile + slot,
            device,
        )

    def context_copies(tile):
        return (
            context_copy(tile, 0, x_next, to_xr),
            context_copy(tile, 1, x_prev, to_xl),
            context_copy(tile, 2, x_far, to_xf),
        )

    def rotated(u, gain, cos, sin):
        normal = u * lax.rsqrt(head_mean(u * u) + EPSILON) * gain
        return normal * cos + half_turn(normal) * sin

    def project(block):
        rows = pl.ds(aligned(block, ROWS), ROWS)

        def pair(tile, carry):
            out = dot(span[block], weights[:, pl.ds(aligned(tile, PAIR), PAIR)])
            for side in range(2):
                u = out[:, side * HEAD : (side + 1) * HEAD]
                head = 2 * tile + side
                u_query[head, rows, :] = u
                turned = rotated(u, q_gain[...], cosine[rows, :], sine[rows, :])
                queries[head, rows, :] = turned.astype(BF16)
                queries_t[head, :, rows] = turned.T.astype(BF16)
            return carry

        lax.fori_loop(0, HEADS // 2, pair, 0)
        out = dot(span[block], weights[:, QUERY_COLUMNS:])
        u = out[:, :HEAD]
        u_key[rows, :] = u
        keys[rows, :] = rotated(u, k_gain[...], cosine[rows, :], sine[rows, :]).astype(BF16)
        values[rows, :] = out[:, HEAD:].astype(BF16)

    def rotated_rows(block):
        return pl.ds(aligned(lax.rem(block - x + 1 + RING_X, RING_X), ROWS), ROWS)

    def transpose_rows(block):
        def chunk(i, carry):
            features = pl.ds(aligned(i, 256), 256)
            span_t[features, rotated_rows(block)] = span[block, :, features].T
            return carry

        lax.fori_loop(0, FEATURES // 256, chunk, 0)

    def transpose_weights():
        def chunk(i, carry):
            features = pl.ds(aligned(i, 256), 256)
            for first in range(0, COLUMNS, PAIR):
                columns = slice(first, first + PAIR)
                weights_t[columns, features] = weights[features, columns].T
            return carry

        lax.fori_loop(0, FEATURES // 256, chunk, 0)

    own_rows.wait()
    for copy in own_weights + tables:
        copy.wait()
    project(x)
    right_low.wait_recv()
    left_high.wait_recv()
    pass_right.start()
    pass_left.start()

    def send_context(tile, carry):
        for copy in context_copies(tile):
            copy.start()
        return carry

    lax.fori_loop(0, TILES - 1, send_context, 0)
    transpose_rows(x)
    transpose_weights()
    right_high.wait_recv()
    project(x_prev)
    left_low.wait_recv()
    project(x_next)
    transpose_rows(x_prev)
    transpose_rows(x_next)
    pass_right.wait_recv()
    pass_left.wait_recv()
    project(x_far)
    transpose_rows(x_far)
    own_context.wait()

    length = lengths[0]

    def norm_gradient(u, gain, grad):
        inverse = lax.rsqrt(head_mean(u * u) + EPSILON)
        weighted = gain * grad
        return inverse * weighted - u * (inverse * inverse * inverse) * head_mean(u * weighted)

    def unrotated(grad, rows):
        return grad * cosine[rows, :] - half_turn(grad) * sine[rows, :]

    def store_grads(first, columns, values):
        low_values = values.astype(BF16)
        for start in range(0, values.shape[0], ROWS):
            target = rotated_rows((first + start) // ROWS)
            grads[target, columns] = low_values[start : start + ROWS]

    def attend(head):
        columns = pl.ds(aligned(head, HEAD), HEAD)
        for first in range(0, SPAN, QUERY_ROWS):
            rows = slice(first, first + QUERY_ROWS)
            seen = first + QUERY_ROWS
            position = lax.broadcasted_iota(jnp.int32, (QUERY_ROWS, 1), 0) + first
            limit = jnp.minimum(position, length - 1)
            key_position = lax.broadcasted_iota(jnp.int32, (QUERY_ROWS, seen), 1)
            key, value = keys[:seen, :], values[:seen, :]
            scores = dot_t(queries[head, rows, :], key)
            weight = jnp.where(key_position <= limit, jnp.exp2(scores * SCORE_SCALE), 0.0)
            probs = weight * (1.0 / jnp.sum(weight, -1, keepdims=True))
            probs_low = probs.astype(BF16)
            context = dot(probs_low, value)
            d_out = jnp.where(position < length, ctx[rows, columns].astype(F32), 0.0)
            d_low = d_out.astype(BF16)
            delta = jnp.sum(d_out * context, -1, keepdims=True)
            d_score = (probs * (dot_t(d_low, value) - delta)).astype(BF16)
            d_query = dot(d_score, key) * SCALE
            store_grads(
                first,
                columns,
                norm_gradient(u_query[head, rows, :], q_gain[...], unrotated(d_query, rows)),
            )
            dk_t[:, :seen] += dot(queries_t[head, :, rows], d_score)
            dv_t[:, :seen] += dot(d_out.T.astype(BF16), probs_low)

    dk_t[...] = jnp.zeros_like(dk_t)
    dv_t[...] = jnp.zeros_like(dv_t)

    def attend_pair(tile):
        for copy in context_copies(tile):
            copy.wait_recv()
        for side in range(2):
            attend(2 * tile + side)

    def key_value_gradients():
        d_key = dk_t[...].T * SCALE
        store_grads(
            0,
            slice(QUERY_COLUMNS, QUERY_COLUMNS + HEAD),
            norm_gradient(u_key[...], k_gain[...], unrotated(d_key, slice(0, SPAN))),
        )
        store_grads(0, slice(QUERY_COLUMNS + HEAD, COLUMNS), dv_t[...].T)

    half = ROWS // 2
    sides = [pl.ds(0, FEATURES // 2), pl.ds(FEATURES // 2, FEATURES // 2)]
    far_copies, near_copies = [], []
    for i, side in enumerate(sides):
        far_copies += [
            remote(dx_far.at[low, side], x_far_r.at[:, side], INPUT + 4 * i, to_xr),
            remote(dx_far.at[high, side], x_far_l.at[:, side], INPUT + 4 * i + 1, to_xl),
        ]
        near_copies += [
            remote(dx_send_r.at[low, side], x_near_r.at[low, side], INPUT + 4 * i + 2, to_xr),
            remote(dx_send_l.at[high, side], x_near_l.at[high, side], INPUT + 4 * i + 3, to_xl),
        ]
    first_copies = [
        remote(dx_send_r.at[high, :], x_near_r.at[high, :], INPUT + 8, to_xr),
        remote(dx_send_l.at[low, :], x_near_l.at[low, :], INPUT + 9, to_xl),
    ]
    chunks = FEATURES // 512

    def input_first(side):
        def chunk(i, carry):
            features = pl.ds(aligned(i, 256), 256)
            out = dot(grads[...], weights_t[:, features])
            dx_far[:, features] = out[3 * ROWS :].astype(BF16)
            dx_wait_l[:, features] = out[half:ROWS]
            dx_send_l[:half, features] = out[:half].astype(BF16)
            dx_own[:, features] = out[ROWS : 2 * ROWS]
            dx_wait_r[:, features] = out[2 * ROWS : 2 * ROWS + half]
            dx_send_r[half:, features] = out[2 * ROWS + half : 3 * ROWS].astype(BF16)
            return carry

        lax.fori_loop(side * chunks, (side + 1) * chunks, chunk, 0)
        for copy in far_copies[2 * side : 2 * side + 2]:
            copy.start()
        if side == 1:
            for copy in first_copies:
                copy.start()

    def input_second(side):
        def chunk(i, carry):
            features = pl.ds(aligned(i, 256), 256)
            dx_send_r[:half, features] = (
                dx_wait_r[:, features] + x_far_r[:, features].astype(F32)
            ).astype(BF16)
            dx_send_l[half:, features] = (
                dx_wait_l[:, features] + x_far_l[:, features].astype(F32)
            ).astype(BF16)
            return carry

        for copy in far_copies[2 * side : 2 * side + 2]:
            copy.wait_recv()
        lax.fori_loop(side * chunks, (side + 1) * chunks, chunk, 0)
        for copy in near_copies[2 * side : 2 * side + 2]:
            copy.start()

    def input_last():
        def chunk(i, carry):
            features = pl.ds(aligned(i, 256), 256)
            dx_out[:, features] = (
                dx_own[:, features]
                + x_near_r[:, features].astype(F32)
                + x_near_l[:, features].astype(F32)
            ).astype(BF16)
            return carry

        for copy in first_copies + near_copies:
            copy.wait_recv()
        lax.fori_loop(0, FEATURES // 256, chunk, 0)

    def core_copy(tile):
        return remote(part_send.at[tile], part_recv.at[tile], CORE + tile, to_core)

    chunk_blocks = 4

    def weight_gradient(tile):
        columns = pl.ds(aligned(tile, PAIR), PAIR)
        by_z = lax.rem(tile + 1, 2) * (1 - lax.div(tile, 4))

        def chunk(i, carry):
            features = pl.ds(aligned(i, chunk_blocks * BLOCK_ROWS), chunk_blocks * BLOCK_ROWS)
            out = dot(span_t[features, :], grads[:, columns])
            kept = jnp.where(core == 0, out[:, :HEAD], out[:, HEAD:]).astype(BF16)
            sent = jnp.where(core == 0, out[:, HEAD:], out[:, :HEAD]).astype(BF16)
            for j in range(chunk_blocks):
                block = chunk_blocks * i + j
                block_z, block_y = lax.rem(block, RING_Z), lax.div(block, RING_Z)
                at = by_z * (block_z * RING_Y + block_y) + (1 - by_z) * block
                rows = slice(j * BLOCK_ROWS, (j + 1) * BLOCK_ROWS)
                part[tile, at] = kept[rows]
                part_send[tile, at] = sent[rows]
            return carry

        lax.fori_loop(0, BLOCKS // chunk_blocks, chunk, 0)
        core_copy(tile).start()

    def add_cores(tile):
        def add(i, carry):
            blocks = pl.ds(i * chunk_blocks, chunk_blocks)
            total = part[tile, blocks].astype(F32) + part_recv[tile, blocks].astype(F32)
            part[tile, blocks] = total.astype(BF16)
            return carry

        core_copy(tile).wait_recv()
        lax.fori_loop(0, BLOCKS // chunk_blocks, add, 0)

    def store_result(tile, total):
        result[0, tile] = total[:SHARE]
        result[1, tile] = total[SHARE:]

    def y_copies(tile):
        slot = RING_SLOT + 10 * tile
        index = STRAIGHT.index(tile)
        return [
            remote(
                part.at[tile, pl.ds(lax.rem(y + k, RING_Y) * RING_Z, RING_Z)],
                y_recv.at[index, k - 1],
                slot + k - 1,
                (place(lax.rem(y + k, RING_Y), z, core), x),
            )
            for k in (1, 2, 3)
        ]

    def z_copies(tile):
        slot = RING_SLOT + 10 * tile + 3
        index = STRAIGHT.index(tile)
        return [
            remote(
                z_send.at[index, k - 1],
                z_recv.at[index, k - 1],
                slot + k - 1,
                (place(y, lax.rem(z + k, RING_Z), core), x),
            )
            for k in range(1, RING_Z)
        ]

    def straight_first(tile):
        add_cores(tile)
        for copy in y_copies(tile):
            copy.start()

    def straight_second(tile):
        index = STRAIGHT.index(tile)
        for copy in y_copies(tile):
            copy.wait_recv()
        copies = z_copies(tile)
        for k in (1, 2, 3, 4, 5, 6, 7, 0):
            block = lax.rem(z + k, RING_Z)
            total = part[tile, y * RING_Z + block].astype(F32)
            for i in range(3):
                total = total + y_recv[index, i, block].astype(F32)
            if k:
                z_send[index, k - 1] = total.astype(BF16)
                copies[k - 1].start()
            else:
                own_total[tile] = total

    def straight_third(tile):
        index = STRAIGHT.index(tile)
        for copy in z_copies(tile):
            copy.wait_recv()
        total = own_total[tile]
        for i in range(RING_Z - 1):
            total = total + z_recv[index, i].astype(F32)
        store_result(tile, total)

    sign = 1 - 2 * core

    def ahead(k):
        return lax.rem(z + RING_Z + sign * k, RING_Z)

    to_long, to_short = (place(y, ahead(1), core), x), (place(y, ahead(-1), core), x)

    def long_copy(tile, step):
        index = RINGED.index(tile)
        return remote(
            long_send.at[index, step], long_recv.at[index, step], RING_SLOT + 10 * tile + step, to_long
        )

    def short_copy(tile, step):
        index = RINGED.index(tile)
        return remote(
            short_send.at[index, step],
            short_recv.at[index, step],
            RING_SLOT + 10 * tile + 4 + step,
            to_short,
        )

    def ring_part(tile, block):
        return part[tile, pl.ds(block * RING_Y, RING_Y)].astype(F32)

    def ring_step(tile, step):
        index = RINGED.index(tile)
        if step == 0:
            add_cores(tile)
        total = ring_part(tile, ahead(4 - step))
        if step > 0:
            long_copy(tile, step - 1).wait_recv()
            total = total + long_recv[index, step - 1].astype(F32)
        long_send[index, step] = total.astype(BF16)
        long_copy(tile, step).start()
        if step < 3:
            total = ring_part(tile, ahead(step - 3))
            if step > 0:
                short_copy(tile, step - 1).wait_recv()
                total = total + short_recv[index, step - 1].astype(F32)
            short_send[index, step] = total.astype(BF16)
            short_copy(tile, step).start()

    def last_copies(tile):
        index = RINGED.index(tile)
        return [
            remote(
                last_send.at[index, k - 1],
                last_recv.at[index, k - 1],
                RING_SLOT + 10 * tile + 7 + k - 1,
                (place(lax.rem(y + k, RING_Y), z, core), x),
            )
            for k in (1, 2, 3)
        ]

    def ring_fifth(tile):
        index = RINGED.index(tile)
        long_copy(tile, 3).wait_recv()
        short_copy(tile, 2).wait_recv()
        copies = last_copies(tile)
        for k in (1, 2, 3, 0):
            block = lax.rem(y + k, RING_Y)
            total = (
                part[tile, z * RING_Y + block].astype(F32)
                + long_recv[index, 3, block].astype(F32)
                + short_recv[index, 2, block].astype(F32)
            )
            if k:
                last_send[index, k - 1] = total.astype(BF16)
                copies[k - 1].start()
            else:
                own_total[tile] = total

    def ring_sixth(tile):
        index = RINGED.index(tile)
        for copy in last_copies(tile):
            copy.wait_recv()
        total = own_total[tile]
        for i in range(3):
            total = total + last_recv[index, i].astype(F32)
        store_result(tile, total)

    def step(turn, carry):
        attend_pair(turn)

        @pl.when(turn < TILES - 2)
        def _():
            weight_gradient(turn)

        @pl.when(turn == 1)
        def _():
            ring_step(0, 0)

        @pl.when(turn == 2)
        def _():
            straight_first(1)
            ring_step(0, 1)

        return carry

    lax.fori_loop(0, TILES - 1, step, 0)
    key_value_gradients()
    input_first(0)
    weight_gradient(3)
    weight_gradient(4)
    input_first(1)
    ring_step(2, 0)
    ring_step(0, 2)
    straight_first(3)
    straight_first(4)
    straight_second(1)
    ring_step(2, 1)
    ring_step(0, 3)
    input_second(0)
    ring_step(2, 2)
    straight_third(1)
    ring_fifth(0)
    input_second(1)
    ring_step(2, 3)
    straight_second(3)
    ring_sixth(0)
    ring_fifth(2)
    straight_second(4)
    straight_third(3)
    ring_sixth(2)
    straight_third(4)

    final = remote(result.at[1 - core], result_recv, FINAL, to_core)
    final.start()
    input_last()
    final.wait_recv()

    mine, other = aligned(core, HEAD), aligned(1 - core, HEAD)
    for tile in range(TILES - 1):
        gq_out[:, pl.ds(tile * PAIR + mine, HEAD)] = result[core, tile]
        gq_out[:, pl.ds(tile * PAIR + other, HEAD)] = result_recv[tile]
    kept, received = result[core, TILES - 1], result_recv[TILES - 1]
    gk_out[...] = jnp.where(core == 0, kept, received)
    gv_out[...] = jnp.where(core == 0, received, kept)

    for copy in (right_low, right_high, left_high, left_low, pass_right, pass_left, final):
        copy.wait_send()
    for copy in far_copies + near_copies + first_copies:
        copy.wait_send()

    def drain_context(tile, carry):
        for copy in context_copies(tile):
            copy.wait_send()
        return carry

    lax.fori_loop(0, TILES - 1, drain_context, 0)
    for tile in range(TILES):
        copies = [core_copy(tile)]
        if tile in RINGED:
            copies += [long_copy(tile, i) for i in range(4)] + [short_copy(tile, i) for i in range(3)]
            copies += last_copies(tile)
        else:
            copies += y_copies(tile) + z_copies(tile)
        for copy in copies:
            copy.wait_send()


def write_results(*refs):
    for source, target in zip(refs[:4], refs[4:]):
        target[...] = source[...]


def local(normed, w_query, key_weight, value_weight, q_gain, key_norm_gain, ctx_grad, lengths):
    cosine, sine = angle_tables()
    block = (BLOCK_ROWS, HEAD)
    vmem = pl.BlockSpec(memory_space=pltpu.VMEM)
    anywhere = pl.BlockSpec(memory_space=pl.ANY)
    smem = pl.BlockSpec(memory_space=pltpu.SMEM)
    scratch = [
        pltpu.VMEM((SPAN, HEAD), F32),
        pltpu.VMEM((SPAN, HEAD), F32),
        pltpu.VMEM((FEATURES, COLUMNS), BF16),
        pltpu.VMEM((COLUMNS, FEATURES), BF16),
        pltpu.VMEM((RING_X, ROWS, FEATURES), BF16),
        pltpu.VMEM((FEATURES, SPAN), BF16),
        pltpu.VMEM((SPAN, QUERY_COLUMNS), BF16),
        pltpu.VMEM((HEADS, SPAN, HEAD), F32),
        pltpu.VMEM((SPAN, HEAD), F32),
        pltpu.VMEM((HEADS, SPAN, HEAD), BF16),
        pltpu.VMEM((HEADS, HEAD, SPAN), BF16),
        pltpu.VMEM((SPAN, HEAD), BF16),
        pltpu.VMEM((SPAN, HEAD), BF16),
        pltpu.VMEM((SPAN, COLUMNS), BF16),
        pltpu.VMEM((HEAD, SPAN), F32),
        pltpu.VMEM((HEAD, SPAN), F32),
        pltpu.VMEM((TILES, BLOCKS) + block, BF16),
        pltpu.VMEM((TILES, BLOCKS) + block, BF16),
        pltpu.VMEM((TILES, BLOCKS) + block, BF16),
        pltpu.VMEM((len(STRAIGHT), 3, RING_Z) + block, BF16),
        pltpu.VMEM((len(STRAIGHT), RING_Z - 1) + block, BF16),
        pltpu.VMEM((len(STRAIGHT), RING_Z - 1) + block, BF16),
        pltpu.VMEM((len(RINGED), 4, RING_Y) + block, BF16),
        pltpu.VMEM((len(RINGED), 4, RING_Y) + block, BF16),
        pltpu.VMEM((len(RINGED), 3, RING_Y) + block, BF16),
        pltpu.VMEM((len(RINGED), 3, RING_Y) + block, BF16),
        pltpu.VMEM((len(RINGED), 3) + block, BF16),
        pltpu.VMEM((len(RINGED), 3) + block, BF16),
        pltpu.VMEM((TILES,) + block, F32),
        pltpu.VMEM((2, TILES, SHARE, HEAD), F32),
        pltpu.VMEM((TILES, SHARE, HEAD), F32),
        pltpu.VMEM((ROWS, FEATURES), BF16),
        pltpu.VMEM((ROWS, FEATURES), BF16),
        pltpu.VMEM((ROWS, FEATURES), BF16),
        pltpu.VMEM((ROWS // 2, FEATURES), F32),
        pltpu.VMEM((ROWS // 2, FEATURES), F32),
        pltpu.VMEM((ROWS, FEATURES), F32),
        pltpu.VMEM((ROWS // 2, FEATURES), BF16),
        pltpu.VMEM((ROWS // 2, FEATURES), BF16),
        pltpu.VMEM((ROWS, FEATURES), BF16),
        pltpu.VMEM((ROWS, FEATURES), BF16),
        pltpu.SemaphoreType.DMA((7,)),
        pltpu.SemaphoreType.DMA((SLOTS,)),
        pltpu.SemaphoreType.DMA((SLOTS,)),
    ]
    out_shape = (
        jax.ShapeDtypeStruct((ROWS, FEATURES), BF16),
        jax.ShapeDtypeStruct((SHARE, QUERY_COLUMNS), F32),
        jax.ShapeDtypeStruct((SHARE, HEAD), F32),
        jax.ShapeDtypeStruct((SHARE, HEAD), F32),
    )
    results = pl.pallas_call(
        kernel,
        out_shape=out_shape,
        in_specs=[anywhere] * 4 + [vmem] * 2 + [anywhere, smem, anywhere, anywhere],
        out_specs=(vmem,) * 4,
        scratch_shapes=scratch,
        compiler_params=pltpu.CompilerParams(
            collective_id=0, has_side_effects=True, vmem_limit_bytes=60 * 2**20
        ),
    )(
        normed,
        w_query,
        key_weight,
        value_weight,
        q_gain.reshape(1, HEAD),
        key_norm_gain.reshape(1, HEAD),
        ctx_grad,
        lengths,
        cosine,
        sine,
    )
    return pl.pallas_call(
        write_results,
        out_shape=out_shape,
        in_specs=[vmem] * 4,
        out_specs=(vmem,) * 4,
    )(*results)


def solution(mesh):
    in_specs = (
        P(("dp", "sp"), None),
        P(None, "sp"),
        P(None, "sp"),
        P(None, "sp"),
        P(),
        P(),
        P(("dp", "sp"), None),
        P("dp"),
    )
    out_specs = (P(("dp", "sp"), None), P("dp", "sp"), P("dp", "sp"), P("dp", "sp"))
    return jax.shard_map(local, mesh=mesh, in_specs=in_specs, out_specs=out_specs, check_vma=False)
```

```python
import math

import jax
import jax.numpy as jnp
import numpy as np
from jax import lax
from jax.experimental import pallas as pl
from jax.experimental.pallas import tpu as pltpu
from jax.sharding import PartitionSpec as P

F32 = jnp.float32
BF16 = jnp.bfloat16
EPSILON = 1e-06
LOG_BASE = math.log(1000000.0)
RING_X, RING_Y, RING_Z = 4, 4, 8
ROWS = 128
SPAN = 512
FEATURES = 2560
HEADS = 8
HEAD = 128
QUERY_COLUMNS = HEADS * HEAD
COLUMNS = QUERY_COLUMNS + 2 * HEAD
PAIR = 2 * HEAD
TILES = COLUMNS // PAIR
BLOCKS = RING_Y * RING_Z
BLOCK_ROWS = FEATURES // BLOCKS
SHARE = BLOCK_ROWS // 2
SCALE = HEAD**-0.5
SCORE_SCALE = SCALE * math.log2(math.e)
QUERY_ROWS = 256
RINGED = (0, 1, 2, 3)
STRAIGHT = (0, 1, 2, 3, 4)
DIRECT = (4,)
PADDED = 48

GATHER = 0
CONTEXT = GATHER + 6
CORE = CONTEXT + 3 * (TILES - 1)
RING_SLOT = CORE + TILES
DIRECT_SLOT = RING_SLOT + 10 * TILES
FINAL = DIRECT_SLOT + 15 * len(DIRECT)
INPUT = FINAL + TILES
SLOTS = INPUT + 22


def angle_tables():
    position = np.arange(SPAN, dtype=np.float32)
    freqs = np.exp(np.arange(HEAD // 2, dtype=np.float32) * np.float32(-2.0 * LOG_BASE / HEAD))
    angles = position[:, None] * freqs.astype(np.float32)[None, :]
    cosine, sine = np.cos(angles), np.sin(angles)
    return (
        np.concatenate([cosine, cosine], 1).astype(np.float32),
        np.concatenate([-sine, sine], 1).astype(np.float32),
    )


def dot(a, b):
    return jnp.dot(a, b, preferred_element_type=F32)


def dot_t(a, b):
    return lax.dot_general(a, b, (((1,), (1,)), ((), ())), preferred_element_type=F32)


def half_turn(a):
    return pltpu.roll(a, HEAD // 2, 1)


def head_mean(a):
    return jnp.sum(a, -1, keepdims=True) * (1.0 / HEAD)


def aligned(index, unit):
    return pl.multiple_of(index * unit, unit)


def kernel(
    normed, w_query, key_weight, value_weight, q_gain, k_gain, ctx_in, lengths, cosine_in, sine_in,
    dx_out, gq_out, gk_out, gv_out,
    cosine, sine, weights, weights_t, span, span_t, ctx, u_query, u_key, queries, queries_t, keys, values,
    grads, dk_t, dv_t,
    part, part_send, part_recv, y_recv, z_send, z_recv,
    long_send, long_recv, short_send, short_recv, last_send, last_recv,
    direct_send, direct_recv, own_total, result, result_recv,
    dx_far, dx_send_r, dx_send_l, dx_wait_r, dx_wait_l, dx_own,
    x_far_r, x_far_l, x_near_r, x_near_l,
    local_sem, send_sem, recv_sem,
):
    dp = lax.axis_index("dp")
    x = lax.axis_index("sp")
    core = lax.rem(dp, 2)
    z = lax.rem(lax.div(dp, 2), RING_Z)
    y = lax.div(dp, 2 * RING_Z)

    def place(y_at, z_at, core_at):
        return (y_at * RING_Z + z_at) * 2 + core_at

    x_next, x_prev, x_far = lax.rem(x + 1, RING_X), lax.rem(x + 3, RING_X), lax.rem(x + 2, RING_X)
    to_xr, to_xl, to_xf = (dp, x_next), (dp, x_prev), (dp, x_far)
    to_core = (place(y, z, 1 - core), x)
    partners = [to_xr, to_xl, to_xf, to_core]
    partners += [(place(lax.rem(y + k, RING_Y), z, core), x) for k in range(1, RING_Y)]
    for core_at in (core, 1 - core):
        partners += [(place(y, lax.rem(z + k, RING_Z), core_at), x) for k in range(1, RING_Z)]

    def remote(src, dst, slot, device):
        return pltpu.make_async_remote_copy(
            src_ref=src,
            dst_ref=dst,
            send_sem=send_sem.at[slot],
            recv_sem=recv_sem.at[slot],
            device_id=device,
            device_id_type=pl.DeviceIdType.MESH,
        )

    own_rows = pltpu.make_async_copy(normed, span.at[x], local_sem.at[0])
    own_weights = [
        pltpu.make_async_copy(w_query, weights.at[:, pl.ds(0, QUERY_COLUMNS)], local_sem.at[1]),
        pltpu.make_async_copy(
            key_weight, weights.at[:, pl.ds(QUERY_COLUMNS, HEAD)], local_sem.at[2]
        ),
        pltpu.make_async_copy(
            value_weight, weights.at[:, pl.ds(QUERY_COLUMNS + HEAD, HEAD)], local_sem.at[3]
        ),
    ]
    own_context = pltpu.make_async_copy(
        ctx_in.at[:, pl.ds(aligned(x, QUERY_COLUMNS), QUERY_COLUMNS)],
        ctx.at[pl.ds(aligned(x, ROWS), ROWS), :],
        local_sem.at[4],
    )
    tables = [
        pltpu.make_async_copy(cosine_in, cosine, local_sem.at[5]),
        pltpu.make_async_copy(sine_in, sine, local_sem.at[6]),
    ]
    own_rows.start()
    for copy in own_weights + tables:
        copy.start()
    own_context.start()

    barrier = pltpu.get_barrier_semaphore()
    for device in partners:
        pl.semaphore_signal(barrier, inc=1, device_id=device, device_id_type=pl.DeviceIdType.MESH)
    pl.semaphore_wait(barrier, len(partners))

    low, high = pl.ds(0, ROWS // 2), pl.ds(ROWS // 2, ROWS // 2)

    def gather_own(slot, half, device):
        return remote(normed.at[half, :], span.at[x, half, :], GATHER + slot, device)

    def gather_pass(slot, owner, half, device):
        return remote(
            span.at[owner, half, :], span.at[owner, half, :], GATHER + slot, device
        )

    right_low, right_high = gather_own(0, low, to_xr), gather_own(1, high, to_xr)
    left_high, left_low = gather_own(2, high, to_xl), gather_own(3, low, to_xl)
    pass_right = gather_pass(4, x_prev, low, to_xr)
    pass_left = gather_pass(5, x_next, high, to_xl)
    right_low.start()
    left_high.start()
    right_high.start()
    left_low.start()

    def context_copy(tile, slot, owner, device):
        start = pl.multiple_of(owner * QUERY_COLUMNS + tile * PAIR, PAIR)
        return remote(
            ctx_in.at[:, pl.ds(start, PAIR)],
            ctx.at[pl.ds(aligned(x, ROWS), ROWS), pl.ds(aligned(tile, PAIR), PAIR)],
            CONTEXT + 3 * tile + slot,
            device,
        )

    def context_copies(tile):
        return (
            context_copy(tile, 0, x_next, to_xr),
            context_copy(tile, 1, x_prev, to_xl),
            context_copy(tile, 2, x_far, to_xf),
        )

    def rotated(u, gain, cos, sin):
        normal = u * lax.rsqrt(head_mean(u * u) + EPSILON) * gain
        return normal * cos + half_turn(normal) * sin

    def project(block):
        rows = pl.ds(aligned(block, ROWS), ROWS)

        def pair(tile, carry):
            out = dot(span[block], weights[:, pl.ds(aligned(tile, PAIR), PAIR)])
            for side in range(2):
                u = out[:, side * HEAD : (side + 1) * HEAD]
                head = 2 * tile + side
                u_query[head, rows, :] = u
                turned = rotated(u, q_gain[...], cosine[rows, :], sine[rows, :])
                queries[head, rows, :] = turned.astype(BF16)
                queries_t[head, :, rows] = turned.T.astype(BF16)
            return carry

        lax.fori_loop(0, HEADS // 2, pair, 0, unroll=True)
        out = dot(span[block], weights[:, QUERY_COLUMNS:])
        u = out[:, :HEAD]
        u_key[rows, :] = u
        keys[rows, :] = rotated(u, k_gain[...], cosine[rows, :], sine[rows, :]).astype(BF16)
        values[rows, :] = out[:, HEAD:].astype(BF16)

    def rotated_rows(block):
        return pl.ds(aligned(lax.rem(block - x + 1 + RING_X, RING_X), ROWS), ROWS)

    def transpose_rows(block):
        def chunk(i, carry):
            features = pl.ds(aligned(i, 256), 256)
            span_t[features, rotated_rows(block)] = span[block, :, features].T
            return carry

        lax.fori_loop(0, FEATURES // 256, chunk, 0)

    def transpose_weights():
        def chunk(i, carry):
            features = pl.ds(aligned(i, 256), 256)
            for first in range(0, COLUMNS, PAIR):
                columns = slice(first, first + PAIR)
                weights_t[columns, features] = weights[features, columns].T
            return carry

        lax.fori_loop(0, FEATURES // 256, chunk, 0)

    own_rows.wait()
    for copy in own_weights + tables:
        copy.wait()
    project(x)
    right_low.wait_recv()
    left_high.wait_recv()
    pass_right.start()
    pass_left.start()

    def send_context(tile, carry):
        for copy in context_copies(tile):
            copy.start()
        return carry

    lax.fori_loop(0, TILES - 1, send_context, 0)
    transpose_rows(x)
    transpose_weights()
    right_high.wait_recv()
    project(x_prev)
    left_low.wait_recv()
    project(x_next)
    transpose_rows(x_prev)
    transpose_rows(x_next)
    pass_right.wait_recv()
    pass_left.wait_recv()
    project(x_far)
    transpose_rows(x_far)
    own_context.wait()

    length = lengths[0]

    def norm_gradient(u, gain, grad):
        inverse = lax.rsqrt(head_mean(u * u) + EPSILON)
        weighted = gain * grad
        return inverse * weighted - u * (inverse * inverse * inverse) * head_mean(u * weighted)

    def unrotated(grad, rows):
        return grad * cosine[rows, :] - half_turn(grad) * sine[rows, :]

    def store_grads(first, columns, values):
        low_values = values.astype(BF16)
        for start in range(0, values.shape[0], ROWS):
            target = rotated_rows((first + start) // ROWS)
            grads[target, columns] = low_values[start : start + ROWS]

    def attend(head, first):
        columns = pl.ds(aligned(head, HEAD), HEAD)
        rows = slice(first, first + QUERY_ROWS)
        seen = first + QUERY_ROWS
        position = lax.broadcasted_iota(jnp.int32, (QUERY_ROWS, 1), 0) + first
        limit = jnp.minimum(position, length - 1)
        key_position = lax.broadcasted_iota(jnp.int32, (QUERY_ROWS, seen), 1)
        key, value = keys[:seen, :], values[:seen, :]
        d_out = jnp.where(position < length, ctx[rows, columns].astype(F32), 0.0)
        scores = dot_t(queries[head, rows, :], key)
        d_probs = dot_t(d_out.astype(BF16), value)
        weight = jnp.where(key_position <= limit, jnp.exp2(scores * SCORE_SCALE), 0.0)
        inverse = 1.0 / jnp.sum(weight, -1, keepdims=True)
        delta = jnp.sum(weight * d_probs, -1, keepdims=True) * inverse
        probs = weight * inverse
        probs_low = probs.astype(BF16)
        d_score = (probs * (d_probs - delta)).astype(BF16)
        d_query = dot(d_score, key) * SCALE
        gradient = norm_gradient(u_query[head, rows, :], q_gain[...], unrotated(d_query, rows))
        store_grads(first, columns, gradient)
        return dot(queries_t[head, :, rows], d_score), dot(d_out.T.astype(BF16), probs_low)

    dk_t[...] = jnp.zeros_like(dk_t)
    dv_t[...] = jnp.zeros_like(dv_t)

    def attend_pair(tile):
        for copy in context_copies(tile):
            copy.wait_recv()
        for first in range(0, SPAN, QUERY_ROWS):
            seen = first + QUERY_ROWS
            sums = [attend(2 * tile + side, first) for side in range(2)]
            dk_t[:, :seen] += sums[0][0] + sums[1][0]
            dv_t[:, :seen] += sums[0][1] + sums[1][1]

    def key_value_gradients():
        d_key = dk_t[...].T * SCALE
        store_grads(
            0,
            slice(QUERY_COLUMNS, QUERY_COLUMNS + HEAD),
            norm_gradient(u_key[...], k_gain[...], unrotated(d_key, slice(0, SPAN))),
        )
        store_grads(0, slice(QUERY_COLUMNS + HEAD, COLUMNS), dv_t[...].T)

    half = ROWS // 2
    pieces = 5
    sides = [pl.ds(i * FEATURES // pieces, FEATURES // pieces) for i in range(pieces)]
    far_copies, near_copies = [], []
    for i, side in enumerate(sides):
        far_copies += [
            remote(dx_far.at[low, side], x_far_r.at[:, side], INPUT + 4 * i, to_xr),
            remote(dx_far.at[high, side], x_far_l.at[:, side], INPUT + 4 * i + 1, to_xl),
        ]
        near_copies += [
            remote(dx_send_r.at[low, side], x_near_r.at[low, side], INPUT + 4 * i + 2, to_xr),
            remote(dx_send_l.at[high, side], x_near_l.at[high, side], INPUT + 4 * i + 3, to_xl),
        ]
    first_copies = [
        remote(dx_send_r.at[high, :], x_near_r.at[high, :], INPUT + 4 * pieces, to_xr),
        remote(dx_send_l.at[low, :], x_near_l.at[low, :], INPUT + 4 * pieces + 1, to_xl),
    ]
    chunks = FEATURES // (256 * pieces)

    def input_first(side):
        def chunk(i, carry):
            features = pl.ds(aligned(i, 256), 256)
            out = dot(grads[...], weights_t[:, features])
            dx_far[:, features] = out[3 * ROWS :].astype(BF16)
            dx_wait_l[:, features] = out[half:ROWS]
            dx_send_l[:half, features] = out[:half].astype(BF16)
            dx_own[:, features] = out[ROWS : 2 * ROWS]
            dx_wait_r[:, features] = out[2 * ROWS : 2 * ROWS + half]
            dx_send_r[half:, features] = out[2 * ROWS + half : 3 * ROWS].astype(BF16)
            return carry

        lax.fori_loop(side * chunks, (side + 1) * chunks, chunk, 0)
        for copy in far_copies[2 * side : 2 * side + 2]:
            copy.start()
        if side == pieces - 1:
            for copy in first_copies:
                copy.start()

    def input_second(side):
        def chunk(i, carry):
            features = pl.ds(aligned(i, 256), 256)
            dx_send_r[:half, features] = (
                dx_wait_r[:, features] + x_far_r[:, features].astype(F32)
            ).astype(BF16)
            dx_send_l[half:, features] = (
                dx_wait_l[:, features] + x_far_l[:, features].astype(F32)
            ).astype(BF16)
            return carry

        for copy in far_copies[2 * side : 2 * side + 2]:
            copy.wait_recv()
        lax.fori_loop(side * chunks, (side + 1) * chunks, chunk, 0)
        for copy in near_copies[2 * side : 2 * side + 2]:
            copy.start()

    def input_last():
        def chunk(i, carry):
            features = pl.ds(aligned(i, 256), 256)
            dx_out[:, features] = (
                dx_own[:, features]
                + x_near_r[:, features].astype(F32)
                + x_near_l[:, features].astype(F32)
            ).astype(BF16)
            return carry

        for copy in first_copies:
            copy.wait_recv()
        for side in range(pieces):
            for copy in near_copies[2 * side : 2 * side + 2]:
                copy.wait_recv()
            lax.fori_loop(side * chunks, (side + 1) * chunks, chunk, 0)

    def core_copy(tile):
        return remote(part_send.at[tile], part_recv.at[tile], CORE + tile, to_core)

    chunk_blocks = 4

    def weight_gradient(tile):
        columns = pl.ds(aligned(tile, PAIR), PAIR)
        split = 1 - lax.div(tile, TILES - 1)

        def place_of(block_y, block_z, by_z):
            return by_z * (block_z * RING_Y + block_y) + (1 - by_z) * (block_y * RING_Z + block_z)

        def chunk(block_y, carry):
            size = chunk_blocks * BLOCK_ROWS
            for first in range(0, RING_Z, chunk_blocks):
                features = pl.ds(aligned(block_y * 2 + first // chunk_blocks, size), size)
                out = dot(span_t[features, :], grads[:, columns])
                kept = jnp.where(core == 0, out[:, :HEAD], out[:, HEAD:]).astype(BF16)
                sent = jnp.where(core == 0, out[:, HEAD:], out[:, :HEAD]).astype(BF16)
                for j in range(chunk_blocks):
                    rows = slice(j * BLOCK_ROWS, (j + 1) * BLOCK_ROWS)
                    part[tile, place_of(block_y, first + j, split * core)] = kept[rows]
                    part_send[tile, place_of(block_y, first + j, split * (1 - core))] = sent[rows]
            return carry

        lax.fori_loop(0, RING_Y, chunk, 0)
        core_copy(tile).start()

    def add_cores(tile):
        def add(i, carry):
            blocks = pl.ds(i * chunk_blocks, chunk_blocks)
            total = part[tile, blocks].astype(F32) + part_recv[tile, blocks].astype(F32)
            part[tile, blocks] = total.astype(BF16)
            return carry

        core_copy(tile).wait_recv()
        lax.fori_loop(0, BLOCKS // chunk_blocks, add, 0)

    def store_result(tile, mine, theirs):
        if tile < TILES - 1:
            gq_out[:, pl.ds(tile * PAIR + aligned(core, HEAD), HEAD)] = mine
            gq_out[:, pl.ds(tile * PAIR + aligned(1 - core, HEAD), HEAD)] = theirs
        else:
            gk_out[...] = jnp.where(core == 0, mine, theirs)
            gv_out[...] = jnp.where(core == 0, theirs, mine)

    def y_copies(tile):
        slot = RING_SLOT + 10 * tile
        index = STRAIGHT.index(tile)
        return [
            remote(
                part.at[tile, pl.ds(lax.rem(y + k, RING_Y) * RING_Z, RING_Z)],
                y_recv.at[index, k - 1],
                slot + k - 1,
                (place(lax.rem(y + k, RING_Y), z, core), x),
            )
            for k in (1, 2, 3)
        ]

    def z_copies(tile):
        slot = RING_SLOT + 10 * tile + 3
        index = STRAIGHT.index(tile)
        return [
            remote(
                z_send.at[index, k - 1],
                z_recv.at[index, k - 1],
                slot + k - 1,
                (place(y, lax.rem(z + k, RING_Z), core), x),
            )
            for k in range(1, RING_Z)
        ]

    def straight_first(tile):
        add_cores(tile)
        for copy in y_copies(tile):
            copy.start()

    def final_copy(tile):
        return remote(result.at[1 - core, tile], result_recv.at[tile], FINAL + tile, to_core)

    def direct_copies(tile):
        index = DIRECT.index(tile)
        copies = []
        for k in range(RING_Z):
            for other in (0, 1):
                if k or other:
                    core_at = core if other == 0 else 1 - core
                    copies.append(
                        remote(
                            direct_send.at[index, k, core_at],
                            direct_recv.at[index, core, k],
                            DIRECT_SLOT + 15 * index + 2 * k + other - 1,
                            (place(y, lax.rem(z + k, RING_Z), core_at), x),
                        )
                    )
        return copies

    def straight_second(tile):
        index = STRAIGHT.index(tile)
        for copy in y_copies(tile):
            copy.wait_recv()
        direct = tile in DIRECT
        copies = direct_copies(tile) if direct else z_copies(tile)
        for k in (1, 2, 3, 4, 5, 6, 7, 0):
            block = lax.rem(z + k, RING_Z)
            total = part[tile, y * RING_Z + block].astype(F32)
            for i in range(3):
                total = total + y_recv[index, i, block].astype(F32)
            if k == 0:
                own_total[tile, 0] = total[:SHARE]
                own_total[tile, 1] = total[SHARE:]
            elif not direct:
                z_send[index, k - 1] = total.astype(BF16)
                copies[k - 1].start()
            if direct:
                at = DIRECT.index(tile)
                padding = jnp.zeros((PADDED - SHARE, HEAD), F32)
                for side in (0, 1):
                    rows = total[side * SHARE : (side + 1) * SHARE]
                    direct_send[at, k, side] = jnp.concatenate([rows, padding]).astype(BF16)
                for copy in copies[2 * k - 1 : 2 * k + 1] if k else copies[:1]:
                    copy.start()

    def straight_third(tile):
        index = STRAIGHT.index(tile)
        if tile in DIRECT:
            at = DIRECT.index(tile)
            for copy in direct_copies(tile):
                copy.wait_recv()
            mine = own_total[tile, core]
            for i in range(1, RING_Z):
                mine = mine + direct_recv[at, core, i].astype(F32)[:SHARE]
            theirs = direct_recv[at, 1 - core, 0].astype(F32)[:SHARE]
            for i in range(1, RING_Z):
                theirs = theirs + direct_recv[at, 1 - core, i].astype(F32)[:SHARE]
            store_result(tile, mine, theirs)
            return
        for copy in z_copies(tile):
            copy.wait_recv()
        for side in (0, 1):
            rows = slice(side * SHARE, (side + 1) * SHARE)
            total = own_total[tile, side]
            for i in range(RING_Z - 1):
                total = total + z_recv[index, i].astype(F32)[rows]
            result[side, tile] = total
        final_copy(tile).start()

    def ahead(tile, k):
        return lax.rem(z + RING_Z + (k if tile % 2 else -k), RING_Z)

    def long_copy(tile, step):
        index = RINGED.index(tile)
        return remote(
            long_send.at[index, step],
            long_recv.at[index, step],
            RING_SLOT + 10 * tile + step,
            (place(y, ahead(tile, 1), core), x),
        )

    def short_copy(tile, step):
        index = RINGED.index(tile)
        return remote(
            short_send.at[index, step],
            short_recv.at[index, step],
            RING_SLOT + 10 * tile + 4 + step,
            (place(y, ahead(tile, -1), core), x),
        )

    def ring_part(tile, block):
        return part[tile, pl.ds(block * RING_Y, RING_Y)].astype(F32)

    def ring_step(tile, step):
        index = RINGED.index(tile)
        if step == 0:
            add_cores(tile)
        total = ring_part(tile, ahead(tile, 4 - step))
        if step > 0:
            long_copy(tile, step - 1).wait_recv()
            total = total + long_recv[index, step - 1].astype(F32)
        long_send[index, step] = total.astype(BF16)
        long_copy(tile, step).start()
        if step < 3:
            total = ring_part(tile, ahead(tile, step - 3))
            if step > 0:
                short_copy(tile, step - 1).wait_recv()
                total = total + short_recv[index, step - 1].astype(F32)
            short_send[index, step] = total.astype(BF16)
            short_copy(tile, step).start()

    def last_copies(tile):
        index = RINGED.index(tile)
        return [
            remote(
                last_send.at[index, k - 1],
                last_recv.at[index, k - 1],
                RING_SLOT + 10 * tile + 7 + k - 1,
                (place(lax.rem(y + k, RING_Y), z, core), x),
            )
            for k in (1, 2, 3)
        ]

    def ring_fifth(tile):
        index = RINGED.index(tile)
        long_copy(tile, 3).wait_recv()
        short_copy(tile, 2).wait_recv()
        copies = last_copies(tile)
        for k in (1, 2, 3, 0):
            block = lax.rem(y + k, RING_Y)
            total = (
                part[tile, z * RING_Y + block].astype(F32)
                + long_recv[index, 3, block].astype(F32)
                + short_recv[index, 2, block].astype(F32)
            )
            if k:
                last_send[index, k - 1] = total.astype(BF16)
                copies[k - 1].start()
            else:
                own_total[tile, 0] = total[:SHARE]
                own_total[tile, 1] = total[SHARE:]

    def ring_sixth(tile):
        index = RINGED.index(tile)
        for copy in last_copies(tile):
            copy.wait_recv()
        for side in (0, 1):
            rows = slice(side * SHARE, (side + 1) * SHARE)
            total = own_total[tile, side]
            for i in range(3):
                total = total + last_recv[index, i].astype(F32)[rows]
            result[side, tile] = total
        final_copy(tile).start()

    def on_cores(straight, ringed):
        @pl.when(core == 0)
        def _():
            for stage, tile in straight:
                (straight_first, straight_second, straight_third)[stage](tile)

        @pl.when(core == 1)
        def _():
            for stage, tile in ringed:
                if stage < 4:
                    ring_step(tile, stage)
                else:
                    (ring_fifth, ring_sixth)[stage - 4](tile)

    def step(turn, carry):
        attend_pair(turn)

        @pl.when(turn < TILES - 2)
        def _():
            weight_gradient(turn)

        for tile in (0, 1):

            @pl.when(turn == tile + 1)
            def _(tile=tile):
                on_cores([(0, tile)], [(0, tile)])

        return carry

    lax.fori_loop(0, TILES - 1, step, 0)
    weight_gradient(3)
    on_cores([(0, 2), (1, 0)], [(0, 2), (1, 0), (1, 1)])
    key_value_gradients()
    input_first(0)
    weight_gradient(4)
    input_first(1)
    on_cores([(0, 3)], [(0, 3)])
    input_first(2)
    input_first(3)
    straight_first(4)
    input_first(4)
    on_cores([(1, 1), (1, 2), (2, 0)], [(2, 0), (2, 1), (1, 2), (1, 3)])
    input_second(0)
    input_second(1)
    input_second(2)
    on_cores([(1, 3), (2, 1)], [(3, 0), (3, 1), (2, 2), (2, 3)])
    input_second(3)
    input_second(4)
    on_cores([(2, 2)], [(4, 0), (4, 1), (3, 2), (3, 3)])
    straight_second(4)
    on_cores([(2, 3)], [(5, 0), (5, 1), (4, 2), (4, 3), (5, 2), (5, 3)])
    for tile in range(TILES):
        if tile not in DIRECT:
            final_copy(tile).wait_recv()
            store_result(tile, result[core, tile], result_recv[tile])
    straight_third(4)
    input_last()

    for copy in (right_low, right_high, left_high, left_low, pass_right, pass_left):
        copy.wait_send()
    for copy in far_copies + near_copies + first_copies:
        copy.wait_send()

    def drain_context(tile, carry):
        for copy in context_copies(tile):
            copy.wait_send()
        return carry

    lax.fori_loop(0, TILES - 1, drain_context, 0)
    def finish(copies):
        for copy in copies:
            copy.wait_send()

    for tile in range(TILES):
        finish([core_copy(tile)])
        if tile in DIRECT:
            finish(y_copies(tile) + direct_copies(tile))
        else:
            finish([final_copy(tile)])

            @pl.when(core == 0)
            def _(tile=tile):
                finish(y_copies(tile) + z_copies(tile))

            @pl.when(core == 1)
            def _(tile=tile):
                finish([long_copy(tile, i) for i in range(4)])
                finish([short_copy(tile, i) for i in range(3)])
                finish(last_copies(tile))


def write_results(*refs):
    for source, target in zip(refs[:4], refs[4:]):
        target[...] = source[...]


def local(normed, w_query, key_weight, value_weight, q_gain, key_norm_gain, ctx_grad, lengths):
    cosine, sine = angle_tables()
    block = (BLOCK_ROWS, HEAD)
    vmem = pl.BlockSpec(memory_space=pltpu.VMEM)
    anywhere = pl.BlockSpec(memory_space=pl.ANY)
    smem = pl.BlockSpec(memory_space=pltpu.SMEM)
    scratch = [
        pltpu.VMEM((SPAN, HEAD), F32),
        pltpu.VMEM((SPAN, HEAD), F32),
        pltpu.VMEM((FEATURES, COLUMNS), BF16),
        pltpu.VMEM((COLUMNS, FEATURES), BF16),
        pltpu.VMEM((RING_X, ROWS, FEATURES), BF16),
        pltpu.VMEM((FEATURES, SPAN), BF16),
        pltpu.VMEM((SPAN, QUERY_COLUMNS), BF16),
        pltpu.VMEM((HEADS, SPAN, HEAD), F32),
        pltpu.VMEM((SPAN, HEAD), F32),
        pltpu.VMEM((HEADS, SPAN, HEAD), BF16),
        pltpu.VMEM((HEADS, HEAD, SPAN), BF16),
        pltpu.VMEM((SPAN, HEAD), BF16),
        pltpu.VMEM((SPAN, HEAD), BF16),
        pltpu.VMEM((SPAN, COLUMNS), BF16),
        pltpu.VMEM((HEAD, SPAN), F32),
        pltpu.VMEM((HEAD, SPAN), F32),
        pltpu.VMEM((TILES, BLOCKS) + block, BF16),
        pltpu.VMEM((TILES, BLOCKS) + block, BF16),
        pltpu.VMEM((TILES, BLOCKS) + block, BF16),
        pltpu.VMEM((len(STRAIGHT), 3, RING_Z) + block, BF16),
        pltpu.VMEM((len(STRAIGHT), RING_Z - 1) + block, BF16),
        pltpu.VMEM((len(STRAIGHT), RING_Z - 1) + block, BF16),
        pltpu.VMEM((len(RINGED), 4, RING_Y) + block, BF16),
        pltpu.VMEM((len(RINGED), 4, RING_Y) + block, BF16),
        pltpu.VMEM((len(RINGED), 3, RING_Y) + block, BF16),
        pltpu.VMEM((len(RINGED), 3, RING_Y) + block, BF16),
        pltpu.VMEM((len(RINGED), 3) + block, BF16),
        pltpu.VMEM((len(RINGED), 3) + block, BF16),
        pltpu.VMEM((len(DIRECT), RING_Z, 2, PADDED, HEAD), BF16),
        pltpu.VMEM((len(DIRECT), 2, RING_Z, PADDED, HEAD), BF16),
        pltpu.VMEM((TILES, 2, SHARE, HEAD), F32),
        pltpu.VMEM((2, TILES, SHARE, HEAD), F32),
        pltpu.VMEM((TILES, SHARE, HEAD), F32),
        pltpu.VMEM((ROWS, FEATURES), BF16),
        pltpu.VMEM((ROWS, FEATURES), BF16),
        pltpu.VMEM((ROWS, FEATURES), BF16),
        pltpu.VMEM((ROWS // 2, FEATURES), F32),
        pltpu.VMEM((ROWS // 2, FEATURES), F32),
        pltpu.VMEM((ROWS, FEATURES), F32),
        pltpu.VMEM((ROWS // 2, FEATURES), BF16),
        pltpu.VMEM((ROWS // 2, FEATURES), BF16),
        pltpu.VMEM((ROWS, FEATURES), BF16),
        pltpu.VMEM((ROWS, FEATURES), BF16),
        pltpu.SemaphoreType.DMA((7,)),
        pltpu.SemaphoreType.DMA((SLOTS,)),
        pltpu.SemaphoreType.DMA((SLOTS,)),
    ]
    out_shape = (
        jax.ShapeDtypeStruct((ROWS, FEATURES), BF16),
        jax.ShapeDtypeStruct((SHARE, QUERY_COLUMNS), F32),
        jax.ShapeDtypeStruct((SHARE, HEAD), F32),
        jax.ShapeDtypeStruct((SHARE, HEAD), F32),
    )
    results = pl.pallas_call(
        kernel,
        out_shape=out_shape,
        in_specs=[anywhere] * 4 + [vmem] * 2 + [anywhere, smem, anywhere, anywhere],
        out_specs=(vmem,) * 4,
        scratch_shapes=scratch,
        compiler_params=pltpu.CompilerParams(
            collective_id=0, has_side_effects=True, vmem_limit_bytes=60 * 2**20
        ),
    )(
        normed,
        w_query,
        key_weight,
        value_weight,
        q_gain.reshape(1, HEAD),
        key_norm_gain.reshape(1, HEAD),
        ctx_grad,
        lengths,
        cosine,
        sine,
    )
    return pl.pallas_call(
        write_results,
        out_shape=out_shape,
        in_specs=[vmem] * 4,
        out_specs=(vmem,) * 4,
    )(*results)


def solution(mesh):
    in_specs = (
        P(("dp", "sp"), None),
        P(None, "sp"),
        P(None, "sp"),
        P(None, "sp"),
        P(),
        P(),
        P(("dp", "sp"), None),
        P("dp"),
    )
    out_specs = (P(("dp", "sp"), None), P("dp", "sp"), P("dp", "sp"), P("dp", "sp"))
    return jax.shard_map(local, mesh=mesh, in_specs=in_specs, out_specs=out_specs, check_vma=False)
```

```python
import math

import jax
import jax.numpy as jnp
import numpy as np
from jax import lax
from jax.experimental import pallas as pl
from jax.experimental.pallas import tpu as pltpu
from jax.sharding import PartitionSpec as P

F32 = jnp.float32
BF16 = jnp.bfloat16
EPSILON = 1e-06
LOG_BASE = math.log(1000000.0)
RING_X, RING_Y, RING_Z = 4, 4, 8
ROWS = 128
SPAN = 512
FEATURES = 2560
HEADS = 8
HEAD = 128
QUERY_COLUMNS = HEADS * HEAD
COLUMNS = QUERY_COLUMNS + 2 * HEAD
PAIR = 2 * HEAD
TILES = COLUMNS // PAIR
BLOCKS = RING_Y * RING_Z
BLOCK_ROWS = FEATURES // BLOCKS
SHARE = BLOCK_ROWS // 2
SCALE = HEAD**-0.5
SCORE_SCALE = SCALE * math.log2(math.e)
QUERY_ROWS = 256
RINGED = (0, 1, 2, 3)
STRAIGHT = (0, 1, 2, 3, 4)
DIRECT = (4,)
PADDED = 48

GATHER = 0
CONTEXT = GATHER + 6
CORE = CONTEXT + 3 * (TILES - 1)
RING_SLOT = CORE + TILES
DIRECT_SLOT = RING_SLOT + 10 * TILES
FINAL = DIRECT_SLOT + 15 * len(DIRECT)
INPUT = FINAL + TILES
SLOTS = INPUT + 22


def angle_tables():
    position = np.arange(SPAN, dtype=np.float32)
    freqs = np.exp(np.arange(HEAD // 2, dtype=np.float32) * np.float32(-2.0 * LOG_BASE / HEAD))
    angles = position[:, None] * freqs.astype(np.float32)[None, :]
    cosine, sine = np.cos(angles), np.sin(angles)
    return (
        np.concatenate([cosine, cosine], 1).astype(np.float32),
        np.concatenate([-sine, sine], 1).astype(np.float32),
    )


def dot(a, b):
    return jnp.dot(a, b, preferred_element_type=F32)


def dot_t(a, b):
    return lax.dot_general(a, b, (((1,), (1,)), ((), ())), preferred_element_type=F32)


def half_turn(a):
    return pltpu.roll(a, HEAD // 2, 1)


def head_mean(a):
    return jnp.sum(a, -1, keepdims=True) * (1.0 / HEAD)


def aligned(index, unit):
    return pl.multiple_of(index * unit, unit)


def kernel(
    normed, w_query, key_weight, value_weight, q_gain, k_gain, ctx_in, lengths, cosine_in, sine_in,
    dx_hbm, gq_hbm, gk_hbm, gv_hbm, dx_out, gq_out, gk_out, gv_out,
    cosine, sine, weights, weights_t, span, span_t, ctx, u_query, u_key, queries, queries_t, keys, values,
    grads, dk_t, dv_t,
    part, part_send, part_recv, y_recv, z_send, z_recv,
    long_send, long_recv, short_send, short_recv, last_send, last_recv,
    direct_send, direct_recv, own_total, result, result_recv,
    dx_far, dx_send_r, dx_send_l, dx_wait_r, dx_wait_l, dx_own,
    x_far_r, x_far_l, x_near_r, x_near_l,
    local_sem, send_sem, recv_sem,
):
    dp = lax.axis_index("dp")
    x = lax.axis_index("sp")
    core = lax.rem(dp, 2)
    z = lax.rem(lax.div(dp, 2), RING_Z)
    y = lax.div(dp, 2 * RING_Z)

    def place(y_at, z_at, core_at):
        return (y_at * RING_Z + z_at) * 2 + core_at

    x_next, x_prev, x_far = lax.rem(x + 1, RING_X), lax.rem(x + 3, RING_X), lax.rem(x + 2, RING_X)
    to_xr, to_xl, to_xf = (dp, x_next), (dp, x_prev), (dp, x_far)
    to_core = (place(y, z, 1 - core), x)
    partners = [to_xr, to_xl, to_xf, to_core]
    partners += [(place(lax.rem(y + k, RING_Y), z, core), x) for k in range(1, RING_Y)]
    for core_at in (core, 1 - core):
        partners += [(place(y, lax.rem(z + k, RING_Z), core_at), x) for k in range(1, RING_Z)]

    def remote(src, dst, slot, device):
        return pltpu.make_async_remote_copy(
            src_ref=src,
            dst_ref=dst,
            send_sem=send_sem.at[slot],
            recv_sem=recv_sem.at[slot],
            device_id=device,
            device_id_type=pl.DeviceIdType.MESH,
        )

    own_rows = pltpu.make_async_copy(normed, span.at[x], local_sem.at[0])
    own_weights = [
        pltpu.make_async_copy(w_query, weights.at[:, pl.ds(0, QUERY_COLUMNS)], local_sem.at[1]),
        pltpu.make_async_copy(
            key_weight, weights.at[:, pl.ds(QUERY_COLUMNS, HEAD)], local_sem.at[2]
        ),
        pltpu.make_async_copy(
            value_weight, weights.at[:, pl.ds(QUERY_COLUMNS + HEAD, HEAD)], local_sem.at[3]
        ),
    ]
    own_context = pltpu.make_async_copy(
        ctx_in.at[:, pl.ds(aligned(x, QUERY_COLUMNS), QUERY_COLUMNS)],
        ctx.at[pl.ds(aligned(x, ROWS), ROWS), :],
        local_sem.at[4],
    )
    tables = [
        pltpu.make_async_copy(cosine_in, cosine, local_sem.at[5]),
        pltpu.make_async_copy(sine_in, sine, local_sem.at[6]),
    ]
    own_rows.start()
    for copy in own_weights + tables:
        copy.start()
    own_context.start()

    barrier = pltpu.get_barrier_semaphore()
    for device in partners:
        pl.semaphore_signal(barrier, inc=1, device_id=device, device_id_type=pl.DeviceIdType.MESH)
    pl.semaphore_wait(barrier, len(partners))

    low, high = pl.ds(0, ROWS // 2), pl.ds(ROWS // 2, ROWS // 2)

    def gather_own(slot, half, device):
        return remote(normed.at[half, :], span.at[x, half, :], GATHER + slot, device)

    def gather_pass(slot, owner, half, device):
        return remote(
            span.at[owner, half, :], span.at[owner, half, :], GATHER + slot, device
        )

    right_low, right_high = gather_own(0, low, to_xr), gather_own(1, high, to_xr)
    left_high, left_low = gather_own(2, high, to_xl), gather_own(3, low, to_xl)
    pass_right = gather_pass(4, x_prev, low, to_xr)
    pass_left = gather_pass(5, x_next, high, to_xl)
    right_low.start()
    left_high.start()
    right_high.start()
    left_low.start()

    def context_copy(tile, slot, owner, device):
        start = pl.multiple_of(owner * QUERY_COLUMNS + tile * PAIR, PAIR)
        return remote(
            ctx_in.at[:, pl.ds(start, PAIR)],
            ctx.at[pl.ds(aligned(x, ROWS), ROWS), pl.ds(aligned(tile, PAIR), PAIR)],
            CONTEXT + 3 * tile + slot,
            device,
        )

    def context_copies(tile):
        return (
            context_copy(tile, 0, x_next, to_xr),
            context_copy(tile, 1, x_prev, to_xl),
            context_copy(tile, 2, x_far, to_xf),
        )

    def rotated(u, gain, cos, sin):
        normal = u * lax.rsqrt(head_mean(u * u) + EPSILON) * gain
        return normal * cos + half_turn(normal) * sin

    def project(block):
        rows = pl.ds(aligned(block, ROWS), ROWS)

        def pair(tile, carry):
            out = dot(span[block], weights[:, pl.ds(aligned(tile, PAIR), PAIR)])
            for side in range(2):
                u = out[:, side * HEAD : (side + 1) * HEAD]
                head = 2 * tile + side
                u_query[head, rows, :] = u
                turned = rotated(u, q_gain[...], cosine[rows, :], sine[rows, :])
                queries[head, rows, :] = turned.astype(BF16)
                queries_t[head, :, rows] = turned.T.astype(BF16)
            return carry

        lax.fori_loop(0, HEADS // 2, pair, 0, unroll=True)
        out = dot(span[block], weights[:, QUERY_COLUMNS:])
        u = out[:, :HEAD]
        u_key[rows, :] = u
        keys[rows, :] = rotated(u, k_gain[...], cosine[rows, :], sine[rows, :]).astype(BF16)
        values[rows, :] = out[:, HEAD:].astype(BF16)

    def rotated_rows(block):
        return pl.ds(aligned(lax.rem(block - x + 1 + RING_X, RING_X), ROWS), ROWS)

    def transpose_rows(block):
        def chunk(i, carry):
            features = pl.ds(aligned(i, 256), 256)
            span_t[features, rotated_rows(block)] = span[block, :, features].T
            return carry

        lax.fori_loop(0, FEATURES // 256, chunk, 0)

    def transpose_weights():
        def chunk(i, carry):
            features = pl.ds(aligned(i, 256), 256)
            for first in range(0, COLUMNS, PAIR):
                columns = slice(first, first + PAIR)
                weights_t[columns, features] = weights[features, columns].T
            return carry

        lax.fori_loop(0, FEATURES // 256, chunk, 0)

    own_rows.wait()
    for copy in own_weights + tables:
        copy.wait()
    project(x)
    right_low.wait_recv()
    left_high.wait_recv()
    pass_right.start()
    pass_left.start()

    def send_context(tile, carry):
        for copy in context_copies(tile):
            copy.start()
        return carry

    lax.fori_loop(0, TILES - 1, send_context, 0)
    transpose_rows(x)
    transpose_weights()
    right_high.wait_recv()
    project(x_prev)
    left_low.wait_recv()
    project(x_next)
    transpose_rows(x_prev)
    transpose_rows(x_next)
    pass_right.wait_recv()
    pass_left.wait_recv()
    project(x_far)
    transpose_rows(x_far)
    own_context.wait()

    length = lengths[0]

    def norm_gradient(u, gain, grad):
        inverse = lax.rsqrt(head_mean(u * u) + EPSILON)
        weighted = gain * grad
        return inverse * weighted - u * (inverse * inverse * inverse) * head_mean(u * weighted)

    def unrotated(grad, rows):
        return grad * cosine[rows, :] - half_turn(grad) * sine[rows, :]

    def store_grads(first, columns, values):
        low_values = values.astype(BF16)
        for start in range(0, values.shape[0], ROWS):
            target = rotated_rows((first + start) // ROWS)
            grads[target, columns] = low_values[start : start + ROWS]

    def attend(head, first):
        columns = pl.ds(aligned(head, HEAD), HEAD)
        rows = slice(first, first + QUERY_ROWS)
        seen = first + QUERY_ROWS
        position = lax.broadcasted_iota(jnp.int32, (QUERY_ROWS, 1), 0) + first
        limit = jnp.minimum(position, length - 1)
        key_position = lax.broadcasted_iota(jnp.int32, (QUERY_ROWS, seen), 1)
        key, value = keys[:seen, :], values[:seen, :]
        d_out = jnp.where(position < length, ctx[rows, columns].astype(F32), 0.0)
        scores = dot_t(queries[head, rows, :], key)
        d_probs = dot_t(d_out.astype(BF16), value)
        weight = jnp.where(key_position <= limit, jnp.exp2(scores * SCORE_SCALE), 0.0)
        inverse = 1.0 / jnp.sum(weight, -1, keepdims=True)
        delta = jnp.sum(weight * d_probs, -1, keepdims=True) * inverse
        probs = weight * inverse
        probs_low = probs.astype(BF16)
        d_score = (probs * (d_probs - delta)).astype(BF16)
        d_query = dot(d_score, key) * SCALE
        gradient = norm_gradient(u_query[head, rows, :], q_gain[...], unrotated(d_query, rows))
        store_grads(first, columns, gradient)
        return dot(queries_t[head, :, rows], d_score), dot(d_out.T.astype(BF16), probs_low)

    dk_t[...] = jnp.zeros_like(dk_t)
    dv_t[...] = jnp.zeros_like(dv_t)

    def attend_pair(tile):
        for copy in context_copies(tile):
            copy.wait_recv()
        for first in range(0, SPAN, QUERY_ROWS):
            seen = first + QUERY_ROWS
            sums = [attend(2 * tile + side, first) for side in range(2)]
            dk_t[:, :seen] += sums[0][0] + sums[1][0]
            dv_t[:, :seen] += sums[0][1] + sums[1][1]

    def key_value_gradients():
        d_key = dk_t[...].T * SCALE
        store_grads(
            0,
            slice(QUERY_COLUMNS, QUERY_COLUMNS + HEAD),
            norm_gradient(u_key[...], k_gain[...], unrotated(d_key, slice(0, SPAN))),
        )
        store_grads(0, slice(QUERY_COLUMNS + HEAD, COLUMNS), dv_t[...].T)

    half = ROWS // 2
    pieces = 5
    sides = [pl.ds(i * FEATURES // pieces, FEATURES // pieces) for i in range(pieces)]
    stores = [
        pltpu.make_async_copy(source, target, local_sem.at[7 + i])
        for i, (source, target) in enumerate(
            [(gq_out, gq_hbm), (gk_out, gk_hbm), (gv_out, gv_hbm)]
            + [(dx_out.at[:, side], dx_hbm.at[:, side]) for side in sides]
        )
    ]
    far_copies, near_copies = [], []
    for i, side in enumerate(sides):
        far_copies += [
            remote(dx_far.at[low, side], x_far_r.at[:, side], INPUT + 4 * i, to_xr),
            remote(dx_far.at[high, side], x_far_l.at[:, side], INPUT + 4 * i + 1, to_xl),
        ]
        near_copies += [
            remote(dx_send_r.at[low, side], x_near_r.at[low, side], INPUT + 4 * i + 2, to_xr),
            remote(dx_send_l.at[high, side], x_near_l.at[high, side], INPUT + 4 * i + 3, to_xl),
        ]
    first_copies = [
        remote(dx_send_r.at[high, :], x_near_r.at[high, :], INPUT + 4 * pieces, to_xr),
        remote(dx_send_l.at[low, :], x_near_l.at[low, :], INPUT + 4 * pieces + 1, to_xl),
    ]
    chunks = FEATURES // (256 * pieces)

    def input_first(side):
        def chunk(i, carry):
            features = pl.ds(aligned(i, 256), 256)
            out = dot(grads[...], weights_t[:, features])
            dx_far[:, features] = out[3 * ROWS :].astype(BF16)
            dx_wait_l[:, features] = out[half:ROWS]
            dx_send_l[:half, features] = out[:half].astype(BF16)
            dx_own[:, features] = out[ROWS : 2 * ROWS]
            dx_wait_r[:, features] = out[2 * ROWS : 2 * ROWS + half]
            dx_send_r[half:, features] = out[2 * ROWS + half : 3 * ROWS].astype(BF16)
            return carry

        lax.fori_loop(side * chunks, (side + 1) * chunks, chunk, 0, unroll=True)
        for copy in far_copies[2 * side : 2 * side + 2]:
            copy.start()
        if side == pieces - 1:
            for copy in first_copies:
                copy.start()

    def input_second(side):
        def chunk(i, carry):
            features = pl.ds(aligned(i, 256), 256)
            dx_send_r[:half, features] = (
                dx_wait_r[:, features] + x_far_r[:, features].astype(F32)
            ).astype(BF16)
            dx_send_l[half:, features] = (
                dx_wait_l[:, features] + x_far_l[:, features].astype(F32)
            ).astype(BF16)
            return carry

        for copy in far_copies[2 * side : 2 * side + 2]:
            copy.wait_recv()
        lax.fori_loop(side * chunks, (side + 1) * chunks, chunk, 0)
        for copy in near_copies[2 * side : 2 * side + 2]:
            copy.start()

    def input_last():
        def chunk(i, carry):
            features = pl.ds(aligned(i, 256), 256)
            dx_out[:, features] = (
                dx_own[:, features]
                + x_near_r[:, features].astype(F32)
                + x_near_l[:, features].astype(F32)
            ).astype(BF16)
            return carry

        for copy in first_copies:
            copy.wait_recv()
        for side in range(pieces):
            for copy in near_copies[2 * side : 2 * side + 2]:
                copy.wait_recv()
            lax.fori_loop(side * chunks, (side + 1) * chunks, chunk, 0)
            stores[3 + side].start()

    def core_copy(tile):
        return remote(part_send.at[tile], part_recv.at[tile], CORE + tile, to_core)

    chunk_blocks = 4

    def weight_gradient(tile):
        columns = pl.ds(aligned(tile, PAIR), PAIR)
        split = 1 - lax.div(tile, TILES - 1)

        def place_of(block_y, block_z, by_z):
            return by_z * (block_z * RING_Y + block_y) + (1 - by_z) * (block_y * RING_Z + block_z)

        def chunk(block_y, carry):
            size = chunk_blocks * BLOCK_ROWS
            for first in range(0, RING_Z, chunk_blocks):
                features = pl.ds(aligned(block_y * 2 + first // chunk_blocks, size), size)
                out = dot(span_t[features, :], grads[:, columns])
                kept = jnp.where(core == 0, out[:, :HEAD], out[:, HEAD:]).astype(BF16)
                sent = jnp.where(core == 0, out[:, HEAD:], out[:, :HEAD]).astype(BF16)
                for j in range(chunk_blocks):
                    rows = slice(j * BLOCK_ROWS, (j + 1) * BLOCK_ROWS)
                    part[tile, place_of(block_y, first + j, split * core)] = kept[rows]
                    part_send[tile, place_of(block_y, first + j, split * (1 - core))] = sent[rows]
            return carry

        lax.fori_loop(0, RING_Y, chunk, 0, unroll=True)
        core_copy(tile).start()

    def add_cores(tile):
        def add(i, carry):
            blocks = pl.ds(i * chunk_blocks, chunk_blocks)
            total = part[tile, blocks].astype(F32) + part_recv[tile, blocks].astype(F32)
            part[tile, blocks] = total.astype(BF16)
            return carry

        core_copy(tile).wait_recv()
        lax.fori_loop(0, BLOCKS // chunk_blocks, add, 0, unroll=2)

    def store_result(tile, mine, theirs):
        if tile < TILES - 1:
            gq_out[:, pl.ds(tile * PAIR + aligned(core, HEAD), HEAD)] = mine
            gq_out[:, pl.ds(tile * PAIR + aligned(1 - core, HEAD), HEAD)] = theirs
        else:
            gk_out[...] = jnp.where(core == 0, mine, theirs)
            gv_out[...] = jnp.where(core == 0, theirs, mine)

    def y_copies(tile):
        slot = RING_SLOT + 10 * tile
        index = STRAIGHT.index(tile)
        return [
            remote(
                part.at[tile, pl.ds(lax.rem(y + k, RING_Y) * RING_Z, RING_Z)],
                y_recv.at[index, k - 1],
                slot + k - 1,
                (place(lax.rem(y + k, RING_Y), z, core), x),
            )
            for k in (1, 2, 3)
        ]

    def z_copies(tile):
        slot = RING_SLOT + 10 * tile + 3
        index = STRAIGHT.index(tile)
        return [
            remote(
                z_send.at[index, k - 1],
                z_recv.at[index, k - 1],
                slot + k - 1,
                (place(y, lax.rem(z + k, RING_Z), core), x),
            )
            for k in range(1, RING_Z)
        ]

    def straight_first(tile):
        add_cores(tile)
        for copy in y_copies(tile):
            copy.start()

    def final_copy(tile):
        return remote(result.at[1 - core, tile], result_recv.at[tile], FINAL + tile, to_core)

    def direct_copies(tile):
        index = DIRECT.index(tile)
        copies = []
        for k in range(RING_Z):
            for other in (0, 1):
                if k or other:
                    core_at = core if other == 0 else 1 - core
                    copies.append(
                        remote(
                            direct_send.at[index, k, core_at],
                            direct_recv.at[index, core, k],
                            DIRECT_SLOT + 15 * index + 2 * k + other - 1,
                            (place(y, lax.rem(z + k, RING_Z), core_at), x),
                        )
                    )
        return copies

    def straight_second(tile):
        index = STRAIGHT.index(tile)
        for copy in y_copies(tile):
            copy.wait_recv()
        direct = tile in DIRECT
        copies = direct_copies(tile) if direct else z_copies(tile)
        for k in (1, 2, 3, 4, 5, 6, 7, 0):
            block = lax.rem(z + k, RING_Z)
            total = part[tile, y * RING_Z + block].astype(F32)
            for i in range(3):
                total = total + y_recv[index, i, block].astype(F32)
            if k == 0:
                own_total[tile, 0] = total[:SHARE]
                own_total[tile, 1] = total[SHARE:]
            elif not direct:
                z_send[index, k - 1] = total.astype(BF16)
                copies[k - 1].start()
            if direct:
                at = DIRECT.index(tile)
                padding = jnp.zeros((PADDED - SHARE, HEAD), F32)
                for side in (0, 1):
                    rows = total[side * SHARE : (side + 1) * SHARE]
                    direct_send[at, k, side] = jnp.concatenate([rows, padding]).astype(BF16)
                for copy in copies[2 * k - 1 : 2 * k + 1] if k else copies[:1]:
                    copy.start()

    def straight_third(tile):
        index = STRAIGHT.index(tile)
        if tile in DIRECT:
            at = DIRECT.index(tile)
            for copy in direct_copies(tile):
                copy.wait_recv()
            mine = own_total[tile, core]
            for i in range(1, RING_Z):
                mine = mine + direct_recv[at, core, i].astype(F32)[:SHARE]
            theirs = direct_recv[at, 1 - core, 0].astype(F32)[:SHARE]
            for i in range(1, RING_Z):
                theirs = theirs + direct_recv[at, 1 - core, i].astype(F32)[:SHARE]
            store_result(tile, mine, theirs)
            return
        for copy in z_copies(tile):
            copy.wait_recv()
        for side in (0, 1):
            rows = slice(side * SHARE, (side + 1) * SHARE)
            total = own_total[tile, side]
            for i in range(RING_Z - 1):
                total = total + z_recv[index, i].astype(F32)[rows]
            result[side, tile] = total
        final_copy(tile).start()

    def ahead(tile, k):
        return lax.rem(z + RING_Z + (k if tile % 2 else -k), RING_Z)

    def long_copy(tile, step):
        index = RINGED.index(tile)
        return remote(
            long_send.at[index, step],
            long_recv.at[index, step],
            RING_SLOT + 10 * tile + step,
            (place(y, ahead(tile, 1), core), x),
        )

    def short_copy(tile, step):
        index = RINGED.index(tile)
        return remote(
            short_send.at[index, step],
            short_recv.at[index, step],
            RING_SLOT + 10 * tile + 4 + step,
            (place(y, ahead(tile, -1), core), x),
        )

    def ring_part(tile, block):
        return part[tile, pl.ds(block * RING_Y, RING_Y)].astype(F32)

    def ring_step(tile, step):
        index = RINGED.index(tile)
        if step == 0:
            add_cores(tile)
        total = ring_part(tile, ahead(tile, 4 - step))
        if step > 0:
            long_copy(tile, step - 1).wait_recv()
            total = total + long_recv[index, step - 1].astype(F32)
        long_send[index, step] = total.astype(BF16)
        long_copy(tile, step).start()
        if step < 3:
            total = ring_part(tile, ahead(tile, step - 3))
            if step > 0:
                short_copy(tile, step - 1).wait_recv()
                total = total + short_recv[index, step - 1].astype(F32)
            short_send[index, step] = total.astype(BF16)
            short_copy(tile, step).start()

    def last_copies(tile):
        index = RINGED.index(tile)
        return [
            remote(
                last_send.at[index, k - 1],
                last_recv.at[index, k - 1],
                RING_SLOT + 10 * tile + 7 + k - 1,
                (place(lax.rem(y + k, RING_Y), z, core), x),
            )
            for k in (1, 2, 3)
        ]

    def ring_fifth(tile):
        index = RINGED.index(tile)
        long_copy(tile, 3).wait_recv()
        short_copy(tile, 2).wait_recv()
        copies = last_copies(tile)
        for k in (1, 2, 3, 0):
            block = lax.rem(y + k, RING_Y)
            total = (
                part[tile, z * RING_Y + block].astype(F32)
                + long_recv[index, 3, block].astype(F32)
                + short_recv[index, 2, block].astype(F32)
            )
            if k:
                last_send[index, k - 1] = total.astype(BF16)
                copies[k - 1].start()
            else:
                own_total[tile, 0] = total[:SHARE]
                own_total[tile, 1] = total[SHARE:]

    def ring_sixth(tile):
        index = RINGED.index(tile)
        for copy in last_copies(tile):
            copy.wait_recv()
        for side in (0, 1):
            rows = slice(side * SHARE, (side + 1) * SHARE)
            total = own_total[tile, side]
            for i in range(3):
                total = total + last_recv[index, i].astype(F32)[rows]
            result[side, tile] = total
        final_copy(tile).start()

    def finish(copies):
        for copy in copies:
            copy.wait_send()

    def finish_tile(tile):
        if tile in DIRECT:
            finish(y_copies(tile) + direct_copies(tile))
            return
        finish([final_copy(tile)])

        @pl.when(core == 0)
        def _():
            finish(y_copies(tile) + z_copies(tile))

        @pl.when(core == 1)
        def _():
            finish([long_copy(tile, i) for i in range(4)])
            finish([short_copy(tile, i) for i in range(3)])
            finish(last_copies(tile))

    def finish_first():
        finish([right_low, right_high, left_high, left_low, pass_right, pass_left])
        for tile in range(TILES - 1):
            finish(context_copies(tile))
        finish(far_copies)

    def on_cores(straight, ringed):
        @pl.when(core == 0)
        def _():
            for stage, tile in straight:
                (straight_first, straight_second, straight_third)[stage](tile)

        @pl.when(core == 1)
        def _():
            for stage, tile in ringed:
                if stage < 4:
                    ring_step(tile, stage)
                else:
                    (ring_fifth, ring_sixth)[stage - 4](tile)

    def step(turn, carry):
        attend_pair(turn)

        @pl.when(turn < TILES - 2)
        def _():
            weight_gradient(turn)

        for tile in (0, 1):

            @pl.when(turn == tile + 1)
            def _(tile=tile):
                on_cores([(0, tile)], [(0, tile)])

        return carry

    lax.fori_loop(0, TILES - 1, step, 0)
    weight_gradient(3)
    on_cores([(0, 2), (1, 0)], [(0, 2), (1, 0), (1, 1)])
    key_value_gradients()
    weight_gradient(4)
    input_first(0)
    input_first(1)
    on_cores([(0, 3)], [(0, 3)])
    input_first(2)
    input_first(3)
    straight_first(4)
    input_first(4)
    on_cores([(1, 1), (1, 2), (2, 0)], [(2, 0), (2, 1), (1, 2), (1, 3)])
    input_second(0)
    input_second(1)
    input_second(2)
    on_cores([(1, 3), (2, 1)], [(3, 0), (3, 1), (2, 2), (2, 3)])
    input_second(3)
    input_second(4)
    on_cores([(2, 2)], [(4, 0), (4, 1), (3, 2), (3, 3)])
    straight_second(4)
    on_cores([(2, 3)], [(5, 0), (5, 1), (4, 2), (4, 3), (5, 2), (5, 3)])
    for tile in range(TILES):
        if tile not in DIRECT:
            final_copy(tile).wait_recv()
            store_result(tile, result[core, tile], result_recv[tile])
    straight_third(4)
    for copy in stores[:3]:
        copy.start()
    input_last()

    finish_first()
    finish([core_copy(tile) for tile in range(TILES)])
    finish(first_copies)
    finish(near_copies)
    for tile in range(TILES):
        finish_tile(tile)
    for copy in stores:
        copy.wait()


def write_results(*refs):
    for source, target in zip(refs[:4], refs[4:]):
        target[...] = source[...]


def local(normed, w_query, key_weight, value_weight, q_gain, key_norm_gain, ctx_grad, lengths):
    cosine, sine = angle_tables()
    block = (BLOCK_ROWS, HEAD)
    vmem = pl.BlockSpec(memory_space=pltpu.VMEM)
    anywhere = pl.BlockSpec(memory_space=pl.ANY)
    smem = pl.BlockSpec(memory_space=pltpu.SMEM)
    scratch = [
        pltpu.VMEM((ROWS, FEATURES), BF16),
        pltpu.VMEM((SHARE, QUERY_COLUMNS), F32),
        pltpu.VMEM((SHARE, HEAD), F32),
        pltpu.VMEM((SHARE, HEAD), F32),
        pltpu.VMEM((SPAN, HEAD), F32),
        pltpu.VMEM((SPAN, HEAD), F32),
        pltpu.VMEM((FEATURES, COLUMNS), BF16),
        pltpu.VMEM((COLUMNS, FEATURES), BF16),
        pltpu.VMEM((RING_X, ROWS, FEATURES), BF16),
        pltpu.VMEM((FEATURES, SPAN), BF16),
        pltpu.VMEM((SPAN, QUERY_COLUMNS), BF16),
        pltpu.VMEM((HEADS, SPAN, HEAD), F32),
        pltpu.VMEM((SPAN, HEAD), F32),
        pltpu.VMEM((HEADS, SPAN, HEAD), BF16),
        pltpu.VMEM((HEADS, HEAD, SPAN), BF16),
        pltpu.VMEM((SPAN, HEAD), BF16),
        pltpu.VMEM((SPAN, HEAD), BF16),
        pltpu.VMEM((SPAN, COLUMNS), BF16),
        pltpu.VMEM((HEAD, SPAN), F32),
        pltpu.VMEM((HEAD, SPAN), F32),
        pltpu.VMEM((TILES, BLOCKS) + block, BF16),
        pltpu.VMEM((TILES, BLOCKS) + block, BF16),
        pltpu.VMEM((TILES, BLOCKS) + block, BF16),
        pltpu.VMEM((len(STRAIGHT), 3, RING_Z) + block, BF16),
        pltpu.VMEM((len(STRAIGHT), RING_Z - 1) + block, BF16),
        pltpu.VMEM((len(STRAIGHT), RING_Z - 1) + block, BF16),
        pltpu.VMEM((len(RINGED), 4, RING_Y) + block, BF16),
        pltpu.VMEM((len(RINGED), 4, RING_Y) + block, BF16),
        pltpu.VMEM((len(RINGED), 3, RING_Y) + block, BF16),
        pltpu.VMEM((len(RINGED), 3, RING_Y) + block, BF16),
        pltpu.VMEM((len(RINGED), 3) + block, BF16),
        pltpu.VMEM((len(RINGED), 3) + block, BF16),
        pltpu.VMEM((len(DIRECT), RING_Z, 2, PADDED, HEAD), BF16),
        pltpu.VMEM((len(DIRECT), 2, RING_Z, PADDED, HEAD), BF16),
        pltpu.VMEM((TILES, 2, SHARE, HEAD), F32),
        pltpu.VMEM((2, TILES, SHARE, HEAD), F32),
        pltpu.VMEM((TILES, SHARE, HEAD), F32),
        pltpu.VMEM((ROWS, FEATURES), BF16),
        pltpu.VMEM((ROWS, FEATURES), BF16),
        pltpu.VMEM((ROWS, FEATURES), BF16),
        pltpu.VMEM((ROWS // 2, FEATURES), F32),
        pltpu.VMEM((ROWS // 2, FEATURES), F32),
        pltpu.VMEM((ROWS, FEATURES), F32),
        pltpu.VMEM((ROWS // 2, FEATURES), BF16),
        pltpu.VMEM((ROWS // 2, FEATURES), BF16),
        pltpu.VMEM((ROWS, FEATURES), BF16),
        pltpu.VMEM((ROWS, FEATURES), BF16),
        pltpu.SemaphoreType.DMA((15,)),
        pltpu.SemaphoreType.DMA((SLOTS,)),
        pltpu.SemaphoreType.DMA((SLOTS,)),
    ]
    out_shape = (
        jax.ShapeDtypeStruct((ROWS, FEATURES), BF16),
        jax.ShapeDtypeStruct((SHARE, QUERY_COLUMNS), F32),
        jax.ShapeDtypeStruct((SHARE, HEAD), F32),
        jax.ShapeDtypeStruct((SHARE, HEAD), F32),
    )
    results = pl.pallas_call(
        kernel,
        out_shape=out_shape,
        in_specs=[anywhere] * 4 + [vmem] * 2 + [anywhere, smem, anywhere, anywhere],
        out_specs=(anywhere,) * 4,
        scratch_shapes=scratch,
        compiler_params=pltpu.CompilerParams(
            collective_id=0, has_side_effects=True, vmem_limit_bytes=60 * 2**20
        ),
    )(
        normed,
        w_query,
        key_weight,
        value_weight,
        q_gain.reshape(1, HEAD),
        key_norm_gain.reshape(1, HEAD),
        ctx_grad,
        lengths,
        cosine,
        sine,
    )
    return pl.pallas_call(
        write_results,
        out_shape=out_shape,
        in_specs=[vmem] * 4,
        out_specs=(vmem,) * 4,
    )(*results)


def solution(mesh):
    in_specs = (
        P(("dp", "sp"), None),
        P(None, "sp"),
        P(None, "sp"),
        P(None, "sp"),
        P(),
        P(),
        P(("dp", "sp"), None),
        P("dp"),
    )
    out_specs = (P(("dp", "sp"), None), P("dp", "sp"), P("dp", "sp"), P("dp", "sp"))
    return jax.shard_map(local, mesh=mesh, in_specs=in_specs, out_specs=out_specs, check_vma=False)
```

```python
import math

import jax
import jax.numpy as jnp
import numpy as np
from jax import lax
from jax.experimental import pallas as pl
from jax.experimental.pallas import tpu as pltpu
from jax.sharding import PartitionSpec as P

F32 = jnp.float32
BF16 = jnp.bfloat16
EPSILON = 1e-06
LOG_BASE = math.log(1000000.0)
RING_X, RING_Y, RING_Z = 4, 4, 8
ROWS = 128
SPAN = 512
FEATURES = 2560
HEADS = 8
HEAD = 128
QUERY_COLUMNS = HEADS * HEAD
COLUMNS = QUERY_COLUMNS + 2 * HEAD
PAIR = 2 * HEAD
TILES = COLUMNS // PAIR
BLOCKS = RING_Y * RING_Z
BLOCK_ROWS = FEATURES // BLOCKS
SHARE = BLOCK_ROWS // 2
SCALE = HEAD**-0.5
SCORE_SCALE = SCALE * math.log2(math.e)
QUERY_ROWS = 256
RINGED = (0, 1, 2, 3)
STRAIGHT = (0, 1, 2, 3, 4)
DIRECT = (4,)
PADDED = 48

GATHER = 0
CONTEXT = GATHER + 6
CORE = CONTEXT + 3 * (TILES - 1)
RING_SLOT = CORE + TILES
DIRECT_SLOT = RING_SLOT + 10 * TILES
FINAL = DIRECT_SLOT + 15 * len(DIRECT)
INPUT = FINAL + TILES
SLOTS = INPUT + 22


def angle_tables():
    position = np.arange(SPAN, dtype=np.float32)
    freqs = np.exp(np.arange(HEAD // 2, dtype=np.float32) * np.float32(-2.0 * LOG_BASE / HEAD))
    angles = position[:, None] * freqs.astype(np.float32)[None, :]
    cosine, sine = np.cos(angles), np.sin(angles)
    return (
        np.concatenate([cosine, cosine], 1).astype(np.float32),
        np.concatenate([-sine, sine], 1).astype(np.float32),
    )


def dot(a, b):
    return jnp.dot(a, b, preferred_element_type=F32)


def dot_t(a, b):
    return lax.dot_general(a, b, (((1,), (1,)), ((), ())), preferred_element_type=F32)


def half_turn(a):
    return pltpu.roll(a, HEAD // 2, 1)


def head_mean(a):
    return jnp.sum(a, -1, keepdims=True) * (1.0 / HEAD)


def aligned(index, unit):
    return pl.multiple_of(index * unit, unit)


def kernel(
    normed, w_query, key_weight, value_weight, q_gain, k_gain, ctx_in, lengths, cosine_in, sine_in,
    dx_hbm, gq_hbm, gk_hbm, gv_hbm, dx_out, gq_out, gk_out, gv_out,
    cosine, sine, weights, weights_t, span, span_t, ctx, u_query, u_key, queries, queries_t, keys, values,
    grads, dk_t, dv_t,
    part, part_send, part_recv, y_recv, z_send, z_recv,
    long_send, long_recv, short_send, short_recv, last_send, last_recv,
    direct_send, direct_recv, own_total, result, result_recv,
    dx_far, dx_send_r, dx_send_l, dx_wait_r, dx_wait_l, dx_own,
    x_far_r, x_far_l, x_near_r, x_near_l,
    local_sem, send_sem, recv_sem,
):
    dp = lax.axis_index("dp")
    x = lax.axis_index("sp")
    core = lax.rem(dp, 2)
    z = lax.rem(lax.div(dp, 2), RING_Z)
    y = lax.div(dp, 2 * RING_Z)

    def place(y_at, z_at, core_at):
        return (y_at * RING_Z + z_at) * 2 + core_at

    x_next, x_prev, x_far = lax.rem(x + 1, RING_X), lax.rem(x + 3, RING_X), lax.rem(x + 2, RING_X)
    to_xr, to_xl, to_xf = (dp, x_next), (dp, x_prev), (dp, x_far)
    to_core = (place(y, z, 1 - core), x)
    partners = [to_xr, to_xl, to_xf, to_core]
    partners += [(place(lax.rem(y + k, RING_Y), z, core), x) for k in range(1, RING_Y)]
    for core_at in (core, 1 - core):
        partners += [(place(y, lax.rem(z + k, RING_Z), core_at), x) for k in range(1, RING_Z)]

    def remote(src, dst, slot, device):
        return pltpu.make_async_remote_copy(
            src_ref=src,
            dst_ref=dst,
            send_sem=send_sem.at[slot],
            recv_sem=recv_sem.at[slot],
            device_id=device,
            device_id_type=pl.DeviceIdType.MESH,
        )

    own_rows = pltpu.make_async_copy(normed, span.at[x], local_sem.at[0])
    own_weights = [
        pltpu.make_async_copy(w_query, weights.at[:, pl.ds(0, QUERY_COLUMNS)], local_sem.at[1]),
        pltpu.make_async_copy(
            key_weight, weights.at[:, pl.ds(QUERY_COLUMNS, HEAD)], local_sem.at[2]
        ),
        pltpu.make_async_copy(
            value_weight, weights.at[:, pl.ds(QUERY_COLUMNS + HEAD, HEAD)], local_sem.at[3]
        ),
    ]
    own_context = pltpu.make_async_copy(
        ctx_in.at[:, pl.ds(aligned(x, QUERY_COLUMNS), QUERY_COLUMNS)],
        ctx.at[pl.ds(aligned(x, ROWS), ROWS), :],
        local_sem.at[4],
    )
    tables = [
        pltpu.make_async_copy(cosine_in, cosine, local_sem.at[5]),
        pltpu.make_async_copy(sine_in, sine, local_sem.at[6]),
    ]
    own_rows.start()
    for copy in own_weights + tables:
        copy.start()
    own_context.start()

    barrier = pltpu.get_barrier_semaphore()
    for device in partners:
        pl.semaphore_signal(barrier, inc=1, device_id=device, device_id_type=pl.DeviceIdType.MESH)
    pl.semaphore_wait(barrier, len(partners))

    low, high = pl.ds(0, ROWS // 2), pl.ds(ROWS // 2, ROWS // 2)

    def gather_own(slot, half, device):
        return remote(normed.at[half, :], span.at[x, half, :], GATHER + slot, device)

    def gather_pass(slot, owner, half, device):
        return remote(
            span.at[owner, half, :], span.at[owner, half, :], GATHER + slot, device
        )

    right_low, right_high = gather_own(0, low, to_xr), gather_own(1, high, to_xr)
    left_high, left_low = gather_own(2, high, to_xl), gather_own(3, low, to_xl)
    pass_right = gather_pass(4, x_prev, low, to_xr)
    pass_left = gather_pass(5, x_next, high, to_xl)
    right_low.start()
    left_high.start()
    right_high.start()
    left_low.start()

    def context_copy(tile, slot, owner, device):
        start = pl.multiple_of(owner * QUERY_COLUMNS + tile * PAIR, PAIR)
        return remote(
            ctx_in.at[:, pl.ds(start, PAIR)],
            ctx.at[pl.ds(aligned(x, ROWS), ROWS), pl.ds(aligned(tile, PAIR), PAIR)],
            CONTEXT + 3 * tile + slot,
            device,
        )

    def context_copies(tile):
        return (
            context_copy(tile, 0, x_next, to_xr),
            context_copy(tile, 1, x_prev, to_xl),
            context_copy(tile, 2, x_far, to_xf),
        )

    def rotated(u, gain, cos, sin):
        normal = u * lax.rsqrt(head_mean(u * u) + EPSILON) * gain
        return normal * cos + half_turn(normal) * sin

    def project(block):
        rows = pl.ds(aligned(block, ROWS), ROWS)

        def pair(tile, carry):
            out = dot(span[block], weights[:, pl.ds(aligned(tile, PAIR), PAIR)])
            for side in range(2):
                u = out[:, side * HEAD : (side + 1) * HEAD]
                head = 2 * tile + side
                u_query[head, rows, :] = u
                turned = rotated(u, q_gain[...], cosine[rows, :], sine[rows, :])
                queries[head, rows, :] = turned.astype(BF16)
                queries_t[head, :, rows] = turned.T.astype(BF16)
            return carry

        lax.fori_loop(0, HEADS // 2, pair, 0, unroll=True)
        out = dot(span[block], weights[:, QUERY_COLUMNS:])
        u = out[:, :HEAD]
        u_key[rows, :] = u
        keys[rows, :] = rotated(u, k_gain[...], cosine[rows, :], sine[rows, :]).astype(BF16)
        values[rows, :] = out[:, HEAD:].astype(BF16)

    def rotated_rows(block):
        return pl.ds(aligned(lax.rem(block - x + 1 + RING_X, RING_X), ROWS), ROWS)

    def transpose_rows(block):
        def chunk(i, carry):
            features = pl.ds(aligned(i, 256), 256)
            span_t[features, rotated_rows(block)] = span[block, :, features].T
            return carry

        lax.fori_loop(0, FEATURES // 256, chunk, 0, unroll=5)

    def transpose_weights():
        def chunk(i, carry):
            features = pl.ds(aligned(i, 256), 256)
            for first in range(0, COLUMNS, PAIR):
                columns = slice(first, first + PAIR)
                weights_t[columns, features] = weights[features, columns].T
            return carry

        lax.fori_loop(0, FEATURES // 256, chunk, 0)

    own_rows.wait()
    for copy in own_weights + tables:
        copy.wait()
    project(x)
    right_low.wait_recv()
    left_high.wait_recv()
    pass_right.start()
    pass_left.start()

    def send_context(tile, carry):
        for copy in context_copies(tile):
            copy.start()
        return carry

    lax.fori_loop(0, TILES - 1, send_context, 0)
    transpose_rows(x)
    transpose_weights()
    right_high.wait_recv()
    project(x_prev)
    left_low.wait_recv()
    project(x_next)
    transpose_rows(x_prev)
    transpose_rows(x_next)
    pass_right.wait_recv()
    pass_left.wait_recv()
    project(x_far)
    transpose_rows(x_far)
    own_context.wait()

    length = lengths[0]

    def norm_gradient(u, gain, grad):
        inverse = lax.rsqrt(head_mean(u * u) + EPSILON)
        weighted = gain * grad
        return inverse * weighted - u * (inverse * inverse * inverse) * head_mean(u * weighted)

    def unrotated(grad, rows):
        return grad * cosine[rows, :] - half_turn(grad) * sine[rows, :]

    def store_grads(first, columns, values):
        low_values = values.astype(BF16)
        for start in range(0, values.shape[0], ROWS):
            target = rotated_rows((first + start) // ROWS)
            grads[target, columns] = low_values[start : start + ROWS]

    def attend(head, first):
        columns = pl.ds(aligned(head, HEAD), HEAD)
        rows = slice(first, first + QUERY_ROWS)
        seen = first + QUERY_ROWS
        position = lax.broadcasted_iota(jnp.int32, (QUERY_ROWS, 1), 0) + first
        limit = jnp.minimum(position, length - 1)
        key_position = lax.broadcasted_iota(jnp.int32, (QUERY_ROWS, seen), 1)
        key, value = keys[:seen, :], values[:seen, :]
        d_out = jnp.where(position < length, ctx[rows, columns].astype(F32), 0.0)
        scores = dot_t(queries[head, rows, :], key)
        d_probs = dot_t(d_out.astype(BF16), value)
        weight = jnp.where(key_position <= limit, jnp.exp2(scores * SCORE_SCALE), 0.0)
        inverse = 1.0 / jnp.sum(weight, -1, keepdims=True)
        delta = jnp.sum(weight * d_probs, -1, keepdims=True) * inverse
        probs = weight * inverse
        probs_low = probs.astype(BF16)
        d_score = (probs * (d_probs - delta)).astype(BF16)
        d_query = dot(d_score, key) * SCALE
        gradient = norm_gradient(u_query[head, rows, :], q_gain[...], unrotated(d_query, rows))
        store_grads(first, columns, gradient)
        return dot(queries_t[head, :, rows], d_score), dot(d_out.T.astype(BF16), probs_low)

    dk_t[...] = jnp.zeros_like(dk_t)
    dv_t[...] = jnp.zeros_like(dv_t)

    def attend_pair(tile):
        for copy in context_copies(tile):
            copy.wait_recv()
        for first in range(0, SPAN, QUERY_ROWS):
            seen = first + QUERY_ROWS
            sums = [attend(2 * tile + side, first) for side in range(2)]
            dk_t[:, :seen] += sums[0][0] + sums[1][0]
            dv_t[:, :seen] += sums[0][1] + sums[1][1]

    def key_value_gradients():
        d_key = dk_t[...].T * SCALE
        store_grads(
            0,
            slice(QUERY_COLUMNS, QUERY_COLUMNS + HEAD),
            norm_gradient(u_key[...], k_gain[...], unrotated(d_key, slice(0, SPAN))),
        )
        store_grads(0, slice(QUERY_COLUMNS + HEAD, COLUMNS), dv_t[...].T)

    half = ROWS // 2
    pieces = 5
    sides = [pl.ds(i * FEATURES // pieces, FEATURES // pieces) for i in range(pieces)]
    stores = [
        pltpu.make_async_copy(source, target, local_sem.at[7 + i])
        for i, (source, target) in enumerate(
            [(gq_out, gq_hbm), (gk_out, gk_hbm), (gv_out, gv_hbm)]
            + [(dx_out.at[:, side], dx_hbm.at[:, side]) for side in sides]
        )
    ]
    far_copies, near_copies = [], []
    for i, side in enumerate(sides):
        far_copies += [
            remote(dx_far.at[low, side], x_far_r.at[:, side], INPUT + 4 * i, to_xr),
            remote(dx_far.at[high, side], x_far_l.at[:, side], INPUT + 4 * i + 1, to_xl),
        ]
        near_copies += [
            remote(dx_send_r.at[low, side], x_near_r.at[low, side], INPUT + 4 * i + 2, to_xr),
            remote(dx_send_l.at[high, side], x_near_l.at[high, side], INPUT + 4 * i + 3, to_xl),
        ]
    first_copies = [
        remote(dx_send_r.at[high, :], x_near_r.at[high, :], INPUT + 4 * pieces, to_xr),
        remote(dx_send_l.at[low, :], x_near_l.at[low, :], INPUT + 4 * pieces + 1, to_xl),
    ]
    chunks = FEATURES // (256 * pieces)

    def input_first(side):
        def chunk(i, carry):
            features = pl.ds(aligned(i, 256), 256)
            out = dot(grads[...], weights_t[:, features])
            dx_far[:, features] = out[3 * ROWS :].astype(BF16)
            dx_wait_l[:, features] = out[half:ROWS]
            dx_send_l[:half, features] = out[:half].astype(BF16)
            dx_own[:, features] = out[ROWS : 2 * ROWS]
            dx_wait_r[:, features] = out[2 * ROWS : 2 * ROWS + half]
            dx_send_r[half:, features] = out[2 * ROWS + half : 3 * ROWS].astype(BF16)
            return carry

        lax.fori_loop(side * chunks, (side + 1) * chunks, chunk, 0, unroll=True)
        for copy in far_copies[2 * side : 2 * side + 2]:
            copy.start()
        if side == pieces - 1:
            for copy in first_copies:
                copy.start()

    def input_second(side):
        def chunk(i, carry):
            features = pl.ds(aligned(i, 256), 256)
            dx_send_r[:half, features] = (
                dx_wait_r[:, features] + x_far_r[:, features].astype(F32)
            ).astype(BF16)
            dx_send_l[half:, features] = (
                dx_wait_l[:, features] + x_far_l[:, features].astype(F32)
            ).astype(BF16)
            return carry

        for copy in far_copies[2 * side : 2 * side + 2]:
            copy.wait_recv()
        lax.fori_loop(side * chunks, (side + 1) * chunks, chunk, 0, unroll=True)
        for copy in near_copies[2 * side : 2 * side + 2]:
            copy.start()

    def input_last():
        def chunk(i, carry):
            features = pl.ds(aligned(i, 256), 256)
            dx_out[:, features] = (
                dx_own[:, features]
                + x_near_r[:, features].astype(F32)
                + x_near_l[:, features].astype(F32)
            ).astype(BF16)
            return carry

        for copy in first_copies:
            copy.wait_recv()
        for side in range(pieces):
            for copy in near_copies[2 * side : 2 * side + 2]:
                copy.wait_recv()
            lax.fori_loop(side * chunks, (side + 1) * chunks, chunk, 0, unroll=True)
            stores[3 + side].start()

    def core_copy(tile):
        return remote(part_send.at[tile], part_recv.at[tile], CORE + tile, to_core)

    chunk_blocks = 4

    def weight_gradient(tile):
        columns = pl.ds(aligned(tile, PAIR), PAIR)
        split = 1 - lax.div(tile, TILES - 1)

        def place_of(block_y, block_z, by_z):
            return by_z * (block_z * RING_Y + block_y) + (1 - by_z) * (block_y * RING_Z + block_z)

        def chunk(block_y, carry):
            size = chunk_blocks * BLOCK_ROWS
            for first in range(0, RING_Z, chunk_blocks):
                features = pl.ds(aligned(block_y * 2 + first // chunk_blocks, size), size)
                out = dot(span_t[features, :], grads[:, columns])
                kept = jnp.where(core == 0, out[:, :HEAD], out[:, HEAD:]).astype(BF16)
                sent = jnp.where(core == 0, out[:, HEAD:], out[:, :HEAD]).astype(BF16)
                for j in range(chunk_blocks):
                    rows = slice(j * BLOCK_ROWS, (j + 1) * BLOCK_ROWS)
                    part[tile, place_of(block_y, first + j, split * core)] = kept[rows]
                    part_send[tile, place_of(block_y, first + j, split * (1 - core))] = sent[rows]
            return carry

        lax.fori_loop(0, RING_Y, chunk, 0, unroll=True)
        core_copy(tile).start()

    def add_cores(tile):
        def add(i, carry):
            blocks = pl.ds(i * chunk_blocks, chunk_blocks)
            total = part[tile, blocks].astype(F32) + part_recv[tile, blocks].astype(F32)
            part[tile, blocks] = total.astype(BF16)
            return carry

        core_copy(tile).wait_recv()
        lax.fori_loop(0, BLOCKS // chunk_blocks, add, 0, unroll=4)

    def store_result(tile, mine, theirs):
        if tile < TILES - 1:
            gq_out[:, pl.ds(tile * PAIR + aligned(core, HEAD), HEAD)] = mine
            gq_out[:, pl.ds(tile * PAIR + aligned(1 - core, HEAD), HEAD)] = theirs
        else:
            gk_out[...] = jnp.where(core == 0, mine, theirs)
            gv_out[...] = jnp.where(core == 0, theirs, mine)

    def y_copies(tile):
        slot = RING_SLOT + 10 * tile
        index = STRAIGHT.index(tile)
        return [
            remote(
                part.at[tile, pl.ds(lax.rem(y + k, RING_Y) * RING_Z, RING_Z)],
                y_recv.at[index, k - 1],
                slot + k - 1,
                (place(lax.rem(y + k, RING_Y), z, core), x),
            )
            for k in (1, 2, 3)
        ]

    def z_copies(tile):
        slot = RING_SLOT + 10 * tile + 3
        index = STRAIGHT.index(tile)
        return [
            remote(
                z_send.at[index, k - 1],
                z_recv.at[index, k - 1],
                slot + k - 1,
                (place(y, lax.rem(z + k, RING_Z), core), x),
            )
            for k in range(1, RING_Z)
        ]

    def straight_first(tile):
        add_cores(tile)
        for copy in y_copies(tile):
            copy.start()

    def final_copy(tile):
        return remote(result.at[1 - core, tile], result_recv.at[tile], FINAL + tile, to_core)

    def direct_copies(tile):
        index = DIRECT.index(tile)
        copies = []
        for k in range(RING_Z):
            for other in (0, 1):
                if k or other:
                    core_at = core if other == 0 else 1 - core
                    copies.append(
                        remote(
                            direct_send.at[index, k, core_at],
                            direct_recv.at[index, core, k],
                            DIRECT_SLOT + 15 * index + 2 * k + other - 1,
                            (place(y, lax.rem(z + k, RING_Z), core_at), x),
                        )
                    )
        return copies

    def straight_second(tile):
        index = STRAIGHT.index(tile)
        for copy in y_copies(tile):
            copy.wait_recv()
        direct = tile in DIRECT
        copies = direct_copies(tile) if direct else z_copies(tile)
        for k in (1, 2, 3, 4, 5, 6, 7, 0):
            block = lax.rem(z + k, RING_Z)
            total = part[tile, y * RING_Z + block].astype(F32)
            for i in range(3):
                total = total + y_recv[index, i, block].astype(F32)
            if k == 0:
                own_total[tile, 0] = total[:SHARE]
                own_total[tile, 1] = total[SHARE:]
            elif not direct:
                z_send[index, k - 1] = total.astype(BF16)
                copies[k - 1].start()
            if direct:
                at = DIRECT.index(tile)
                padding = jnp.zeros((PADDED - SHARE, HEAD), F32)
                for side in (0, 1):
                    rows = total[side * SHARE : (side + 1) * SHARE]
                    direct_send[at, k, side] = jnp.concatenate([rows, padding]).astype(BF16)
                for copy in copies[2 * k - 1 : 2 * k + 1] if k else copies[:1]:
                    copy.start()

    def straight_third(tile):
        index = STRAIGHT.index(tile)
        if tile in DIRECT:
            at = DIRECT.index(tile)
            for copy in direct_copies(tile):
                copy.wait_recv()
            mine = own_total[tile, core]
            for i in range(1, RING_Z):
                mine = mine + direct_recv[at, core, i].astype(F32)[:SHARE]
            theirs = direct_recv[at, 1 - core, 0].astype(F32)[:SHARE]
            for i in range(1, RING_Z):
                theirs = theirs + direct_recv[at, 1 - core, i].astype(F32)[:SHARE]
            store_result(tile, mine, theirs)
            return
        for copy in z_copies(tile):
            copy.wait_recv()
        for side in (0, 1):
            rows = slice(side * SHARE, (side + 1) * SHARE)
            total = own_total[tile, side]
            for i in range(RING_Z - 1):
                total = total + z_recv[index, i].astype(F32)[rows]
            result[side, tile] = total
        final_copy(tile).start()

    def ahead(tile, k):
        return lax.rem(z + RING_Z + (k if tile % 2 else -k), RING_Z)

    def long_copy(tile, step):
        index = RINGED.index(tile)
        return remote(
            long_send.at[index, step],
            long_recv.at[index, step],
            RING_SLOT + 10 * tile + step,
            (place(y, ahead(tile, 1), core), x),
        )

    def short_copy(tile, step):
        index = RINGED.index(tile)
        return remote(
            short_send.at[index, step],
            short_recv.at[index, step],
            RING_SLOT + 10 * tile + 4 + step,
            (place(y, ahead(tile, -1), core), x),
        )

    def ring_part(tile, block):
        return part[tile, pl.ds(block * RING_Y, RING_Y)].astype(F32)

    def ring_step(tile, step):
        index = RINGED.index(tile)
        if step == 0:
            add_cores(tile)
        total = ring_part(tile, ahead(tile, 4 - step))
        if step > 0:
            long_copy(tile, step - 1).wait_recv()
            total = total + long_recv[index, step - 1].astype(F32)
        long_send[index, step] = total.astype(BF16)
        long_copy(tile, step).start()
        if step < 3:
            total = ring_part(tile, ahead(tile, step - 3))
            if step > 0:
                short_copy(tile, step - 1).wait_recv()
                total = total + short_recv[index, step - 1].astype(F32)
            short_send[index, step] = total.astype(BF16)
            short_copy(tile, step).start()

    def last_copies(tile):
        index = RINGED.index(tile)
        return [
            remote(
                last_send.at[index, k - 1],
                last_recv.at[index, k - 1],
                RING_SLOT + 10 * tile + 7 + k - 1,
                (place(lax.rem(y + k, RING_Y), z, core), x),
            )
            for k in (1, 2, 3)
        ]

    def ring_fifth(tile):
        index = RINGED.index(tile)
        long_copy(tile, 3).wait_recv()
        short_copy(tile, 2).wait_recv()
        copies = last_copies(tile)
        for k in (1, 2, 3, 0):
            block = lax.rem(y + k, RING_Y)
            total = (
                part[tile, z * RING_Y + block].astype(F32)
                + long_recv[index, 3, block].astype(F32)
                + short_recv[index, 2, block].astype(F32)
            )
            if k:
                last_send[index, k - 1] = total.astype(BF16)
                copies[k - 1].start()
            else:
                own_total[tile, 0] = total[:SHARE]
                own_total[tile, 1] = total[SHARE:]

    def ring_sixth(tile):
        index = RINGED.index(tile)
        for copy in last_copies(tile):
            copy.wait_recv()
        for side in (0, 1):
            rows = slice(side * SHARE, (side + 1) * SHARE)
            total = own_total[tile, side]
            for i in range(3):
                total = total + last_recv[index, i].astype(F32)[rows]
            result[side, tile] = total
        final_copy(tile).start()

    def finish(copies):
        for copy in copies:
            copy.wait_send()

    def finish_tile(tile):
        if tile in DIRECT:
            finish(y_copies(tile) + direct_copies(tile))
            return
        finish([final_copy(tile)])

        @pl.when(core == 0)
        def _():
            finish(y_copies(tile) + z_copies(tile))

        @pl.when(core == 1)
        def _():
            finish([long_copy(tile, i) for i in range(4)])
            finish([short_copy(tile, i) for i in range(3)])
            finish(last_copies(tile))

    def finish_first():
        finish([right_low, right_high, left_high, left_low, pass_right, pass_left])
        for tile in range(TILES - 1):
            finish(context_copies(tile))
        finish(far_copies)

    def on_cores(straight, ringed):
        @pl.when(core == 0)
        def _():
            for stage, tile in straight:
                (straight_first, straight_second, straight_third)[stage](tile)

        @pl.when(core == 1)
        def _():
            for stage, tile in ringed:
                if stage < 4:
                    ring_step(tile, stage)
                else:
                    (ring_fifth, ring_sixth)[stage - 4](tile)

    def step(turn, carry):
        attend_pair(turn)

        @pl.when(turn < TILES - 2)
        def _():
            weight_gradient(turn)

        for tile in (0, 1):

            @pl.when(turn == tile + 1)
            def _(tile=tile):
                on_cores([(0, tile)], [(0, tile)])

        return carry

    lax.fori_loop(0, TILES - 1, step, 0)
    weight_gradient(3)
    on_cores([(0, 2), (1, 0)], [(0, 2), (1, 0), (1, 1)])
    key_value_gradients()
    weight_gradient(4)
    input_first(0)
    input_first(1)
    on_cores([(0, 3)], [(0, 3)])
    input_first(2)
    input_first(3)
    straight_first(4)
    input_first(4)
    on_cores([(1, 1), (1, 2), (2, 0)], [(2, 0), (2, 1), (1, 2), (1, 3)])
    input_second(0)
    input_second(1)
    input_second(2)
    on_cores([(1, 3), (2, 1)], [(3, 0), (3, 1), (2, 2), (2, 3)])
    input_second(3)
    input_second(4)
    on_cores([(2, 2)], [(4, 0), (4, 1), (3, 2), (3, 3)])
    straight_second(4)
    on_cores([(2, 3)], [(5, 0), (5, 1), (4, 2), (4, 3), (5, 2), (5, 3)])
    for tile in range(TILES):
        if tile not in DIRECT:
            final_copy(tile).wait_recv()
            store_result(tile, result[core, tile], result_recv[tile])
    straight_third(4)
    for copy in stores[:3]:
        copy.start()
    input_last()

    finish_first()
    finish([core_copy(tile) for tile in range(TILES)])
    finish(first_copies)
    finish(near_copies)
    for tile in range(TILES):
        finish_tile(tile)
    for copy in stores:
        copy.wait()


def write_results(*refs):
    for source, target in zip(refs[:4], refs[4:]):
        target[...] = source[...]


def local(normed, w_query, key_weight, value_weight, q_gain, key_norm_gain, ctx_grad, lengths):
    cosine, sine = angle_tables()
    block = (BLOCK_ROWS, HEAD)
    vmem = pl.BlockSpec(memory_space=pltpu.VMEM)
    anywhere = pl.BlockSpec(memory_space=pl.ANY)
    smem = pl.BlockSpec(memory_space=pltpu.SMEM)
    scratch = [
        pltpu.VMEM((ROWS, FEATURES), BF16),
        pltpu.VMEM((SHARE, QUERY_COLUMNS), F32),
        pltpu.VMEM((SHARE, HEAD), F32),
        pltpu.VMEM((SHARE, HEAD), F32),
        pltpu.VMEM((SPAN, HEAD), F32),
        pltpu.VMEM((SPAN, HEAD), F32),
        pltpu.VMEM((FEATURES, COLUMNS), BF16),
        pltpu.VMEM((COLUMNS, FEATURES), BF16),
        pltpu.VMEM((RING_X, ROWS, FEATURES), BF16),
        pltpu.VMEM((FEATURES, SPAN), BF16),
        pltpu.VMEM((SPAN, QUERY_COLUMNS), BF16),
        pltpu.VMEM((HEADS, SPAN, HEAD), F32),
        pltpu.VMEM((SPAN, HEAD), F32),
        pltpu.VMEM((HEADS, SPAN, HEAD), BF16),
        pltpu.VMEM((HEADS, HEAD, SPAN), BF16),
        pltpu.VMEM((SPAN, HEAD), BF16),
        pltpu.VMEM((SPAN, HEAD), BF16),
        pltpu.VMEM((SPAN, COLUMNS), BF16),
        pltpu.VMEM((HEAD, SPAN), F32),
        pltpu.VMEM((HEAD, SPAN), F32),
        pltpu.VMEM((TILES, BLOCKS) + block, BF16),
        pltpu.VMEM((TILES, BLOCKS) + block, BF16),
        pltpu.VMEM((TILES, BLOCKS) + block, BF16),
        pltpu.VMEM((len(STRAIGHT), 3, RING_Z) + block, BF16),
        pltpu.VMEM((len(STRAIGHT), RING_Z - 1) + block, BF16),
        pltpu.VMEM((len(STRAIGHT), RING_Z - 1) + block, BF16),
        pltpu.VMEM((len(RINGED), 4, RING_Y) + block, BF16),
        pltpu.VMEM((len(RINGED), 4, RING_Y) + block, BF16),
        pltpu.VMEM((len(RINGED), 3, RING_Y) + block, BF16),
        pltpu.VMEM((len(RINGED), 3, RING_Y) + block, BF16),
        pltpu.VMEM((len(RINGED), 3) + block, BF16),
        pltpu.VMEM((len(RINGED), 3) + block, BF16),
        pltpu.VMEM((len(DIRECT), RING_Z, 2, PADDED, HEAD), BF16),
        pltpu.VMEM((len(DIRECT), 2, RING_Z, PADDED, HEAD), BF16),
        pltpu.VMEM((TILES, 2, SHARE, HEAD), F32),
        pltpu.VMEM((2, TILES, SHARE, HEAD), F32),
        pltpu.VMEM((TILES, SHARE, HEAD), F32),
        pltpu.VMEM((ROWS, FEATURES), BF16),
        pltpu.VMEM((ROWS, FEATURES), BF16),
        pltpu.VMEM((ROWS, FEATURES), BF16),
        pltpu.VMEM((ROWS // 2, FEATURES), F32),
        pltpu.VMEM((ROWS // 2, FEATURES), F32),
        pltpu.VMEM((ROWS, FEATURES), F32),
        pltpu.VMEM((ROWS // 2, FEATURES), BF16),
        pltpu.VMEM((ROWS // 2, FEATURES), BF16),
        pltpu.VMEM((ROWS, FEATURES), BF16),
        pltpu.VMEM((ROWS, FEATURES), BF16),
        pltpu.SemaphoreType.DMA((15,)),
        pltpu.SemaphoreType.DMA((SLOTS,)),
        pltpu.SemaphoreType.DMA((SLOTS,)),
    ]
    out_shape = (
        jax.ShapeDtypeStruct((ROWS, FEATURES), BF16),
        jax.ShapeDtypeStruct((SHARE, QUERY_COLUMNS), F32),
        jax.ShapeDtypeStruct((SHARE, HEAD), F32),
        jax.ShapeDtypeStruct((SHARE, HEAD), F32),
    )
    results = pl.pallas_call(
        kernel,
        out_shape=out_shape,
        in_specs=[anywhere] * 4 + [vmem] * 2 + [anywhere, smem, anywhere, anywhere],
        out_specs=(anywhere,) * 4,
        scratch_shapes=scratch,
        compiler_params=pltpu.CompilerParams(
            collective_id=0, has_side_effects=True, vmem_limit_bytes=60 * 2**20
        ),
    )(
        normed,
        w_query,
        key_weight,
        value_weight,
        q_gain.reshape(1, HEAD),
        key_norm_gain.reshape(1, HEAD),
        ctx_grad,
        lengths,
        cosine,
        sine,
    )
    return pl.pallas_call(
        write_results,
        out_shape=out_shape,
        in_specs=[vmem] * 4,
        out_specs=(vmem,) * 4,
    )(*results)


def solution(mesh):
    in_specs = (
        P(("dp", "sp"), None),
        P(None, "sp"),
        P(None, "sp"),
        P(None, "sp"),
        P(),
        P(),
        P(("dp", "sp"), None),
        P("dp"),
    )
    out_specs = (P(("dp", "sp"), None), P("dp", "sp"), P("dp", "sp"), P("dp", "sp"))
    return jax.shard_map(local, mesh=mesh, in_specs=in_specs, out_specs=out_specs, check_vma=False)
```
